32 devices in a mesh: band: 4 (over x, core), dom: 8 (over z, y).
Axes of the slice: x: 2, y: 2, z: 4, core: 2. Of those that a mesh axis runs over, the one named last changes fastest.
Arguments:
- occupied: float32 [256, 12288], P('band', 'dom'), may hold values from -6 to 6
- start_guess: float32 [1, 256, 12288], P(None, 'band', 'dom'), may hold values from -0.6 to 0.6
- potential: float32 [12288], P('dom'), may hold values from 0.5 to 8
- perturbation: float32 [1, 12288], P(None, 'dom'), may hold values from -6 to 6
- band_energy: float32 [256], P('band'), may hold values from -4 to -0.5
- beta_radial: float32 [512], replicated, may hold values from -0.25 to 0.25
- beta_slope: float32 [512], replicated, may hold values from -0.25 to 0.25
- atom_owner: int32 [32], replicated, may hold values from 0 to 7, as said below
- atom_site: int32 [3, 32], replicated, may hold values from 0 to 15, as said below
- sphere_offset: int32 [3, 512], replicated, may hold values from -5 to 5
- displaced: int32 [1], replicated, may hold values from 0 to 31
Outputs:
- solution: float32 [1, 256, 12288], P(None, 'band', 'dom')
- residual: float32 [1, 256, 12288], P(None, 'band', 'dom')
The draws below stay inside these ranges and needn't reach their ends.
Inputs may be any that keep to these rules, and one draw needn't show every extreme that they name: `atom_owner`: each slab owns at most 8 atoms and some slab owns exactly 8. `atom_site`: row 0 lies below 6, row 1 below 16, row 2 below 16. Atom 0 sits on plane 5 of its slab, row 15 and column 15; atom 1 on plane 0, row 0 and column 0.
All inputs are finite; a program needn't handle non-finite values.
Results may differ from the reference program's by a relative error of at most 0.0003.
Values sent between devices are 32-bit elements; how exact they have to be, the bound alone decides.
A program may use at most 128 MiB of HBM per device.

```python
import math
import jax
import jax.numpy as jnp
from jax import lax

NOCC = 256
NPERT = 1
CZ = 6
NY = 16
NX = 16
ITERS = 2
RAD = 5
PTS = 512
NZ = 48
NCELLS = 12288
NATOM = 32
MOST = 8


def draw_atom_owner(key, part):
    base_key = jax.random.fold_in(key, 11)
    slab_total = NZ // CZ
    busiest = jax.random.randint(jax.random.fold_in(base_key, 1), (), 0, slab_total).astype(jnp.int32)
    slots = jax.random.permutation(jax.random.fold_in(base_key, 2), (slab_total - 1) * MOST)[:NATOM - MOST]
    others = (slots // MOST).astype(jnp.int32)
    others = others + (others >= busiest).astype(jnp.int32)
    owners = jnp.concatenate([jnp.zeros((MOST,), jnp.int32) + busiest, others])
    return jax.random.permutation(jax.random.fold_in(base_key, 3), owners).astype(jnp.int32)


def draw_atom_site(key, part):
    base_key = jax.random.fold_in(key, 23)
    planes = jax.random.randint(jax.random.fold_in(base_key, 1), (NATOM,), 0, CZ)
    row_index = jax.random.randint(jax.random.fold_in(base_key, 2), (NATOM,), 0, NY)
    column_index = jax.random.randint(jax.random.fold_in(base_key, 3), (NATOM,), 0, NX)
    planes = planes.at[0].set(CZ - 1).at[1].set(0)
    row_index = row_index.at[0].set(NY - 1).at[1].set(0)
    column_index = column_index.at[0].set(NX - 1).at[1].set(0)
    return jnp.stack([planes, row_index, column_index]).astype(jnp.int32)


def draw_sphere_offset(key, part):
    base_key = jax.random.fold_in(key, 37)
    offsets = jax.random.randint(base_key, (3, PTS), -RAD, RAD + 1).astype(jnp.int32)
    offsets = offsets.at[0, 0].set(-RAD)
    offsets = offsets.at[0, 1].set(RAD)
    return offsets.astype(jnp.int32)


def shard_levels(own_key, dims, cuts, smallest, high):
    def one(axis_at, blocks):
        draws = jax.random.uniform(jax.random.fold_in(jax.random.fold_in(own_key, 6), axis_at), (blocks,), jnp.float32, smallest / len(cuts), high / len(cuts))
        return jnp.repeat(jnp.exp(draws), dims[axis_at] // blocks).reshape((-1,) + (1,) * (len(dims) - axis_at - 1))

    factor_of = one(*cuts[0])
    for cut in cuts[1:]:
        factor_of = factor_of * one(*cut)
    return factor_of


def centred(key, extent, scale, reach, pieces=(), held_as=jnp.bfloat16):
    factor_of = shard_levels(key, extent, pieces, -0.22, 0.18) if pieces else 1.0
    entries = jax.random.normal(key, extent, jnp.float32) * scale * factor_of
    return jnp.minimum(jnp.maximum(entries, -reach), reach).astype(held_as)


def setup_inputs(seed: int = 0) -> dict:
    streams_of = jax.random.split(jax.random.key(seed), 12)
    return {
        "occupied": centred(streams_of[0], (NOCC, NCELLS), 1.0, 6.0, ((0, 4), (1, 8)), jnp.float32),
        "start_guess": centred(streams_of[1], (NPERT, NOCC, NCELLS), 0.1, 0.6, ((1, 4), (2, 8)), jnp.float32),
        "potential": jnp.clip(jnp.exp(math.log(8.0) - 2.7725887 * jax.random.uniform(streams_of[2], (NCELLS,), jnp.float32) ** shard_levels(streams_of[2], (NCELLS,), ((0, 8),), -0.2, 0.2)), 0.5, 8.0),
        "perturbation": centred(streams_of[3], (NPERT, NCELLS), 1.0, 6.0, ((1, 8),), jnp.float32),
        "band_energy": jnp.clip(-4.0 + 3.5 * jax.random.uniform(streams_of[4], (NOCC,), jnp.float32) ** shard_levels(streams_of[4], (NOCC,), ((0, 4),), -0.2, 0.2), -4.0, -0.5),
        "beta_radial": centred(streams_of[5], (PTS,), PTS ** -0.5, 0.25, (), jnp.float32),
        "beta_slope": centred(streams_of[6], (PTS,), PTS ** -0.5, 0.25, (), jnp.float32),
        "atom_owner": draw_atom_owner(jax.random.fold_in(streams_of[11], 71), 0),
        "atom_site": draw_atom_site(jax.random.fold_in(streams_of[11], 71), 0),
        "sphere_offset": draw_sphere_offset(jax.random.fold_in(streams_of[11], 71), 0),
        "displaced": jax.random.randint(streams_of[10], (NPERT,), 0, NATOM).astype(jnp.int32),
    }


COEF = (-5369.0 / 1800.0, 12.0 / 7.0, -15.0 / 56.0, 10.0 / 189.0, -1.0 / 112.0, 2.0 / 825.0, -1.0 / 1386.0)
KINETIC = 2.0
SHIFT = 20.0
STRENGTH = 10.0
HIGH = lax.Precision.HIGHEST


def kinetic_part(field):
    grid = field.reshape(NPERT, NOCC, NZ, NY, NX)
    total = 3.0 * COEF[0] * grid
    for axis_number in (2, 3, 4):
        for distance in range(1, len(COEF)):
            total = total + COEF[distance] * (jnp.roll(grid, distance, axis_number) + jnp.roll(grid, -distance, axis_number))
    return (-KINETIC * total).reshape(field.shape)


def point_index(atom_owner, atom_site, sphere_offset):
    planes = ((atom_owner * CZ + atom_site[0])[:, None] + sphere_offset[0][None, :]) % NZ
    row_index = (atom_site[1][:, None] + sphere_offset[1][None, :]) % NY
    column_index = (atom_site[2][:, None] + sphere_offset[2][None, :]) % NX
    return ((planes * NY + row_index) * NX + column_index).astype(jnp.int32)


def nonlocal_part(field, point_cell, beta_radial):
    def per_layer(layer_field):
        values = layer_field[:, point_cell]
        projection = jnp.einsum("bak,k->ba", values, beta_radial, precision=HIGH)
        update = STRENGTH * projection[:, :, None] * beta_radial[None, None, :]
        return jnp.zeros_like(layer_field).at[:, point_cell].add(update)
    return lax.map(per_layer, field)


def occupied_part(field, occupied):
    flat_field = field.reshape(-1, NCELLS)
    correlation = jnp.dot(occupied, flat_field.T, precision=HIGH, preferred_element_type=jnp.float32)
    back = jnp.dot(correlation.T, occupied, precision=HIGH, preferred_element_type=jnp.float32)
    return (back / NCELLS).reshape(field.shape)


def reference(occupied, start_guess, potential, perturbation, band_energy, beta_radial, beta_slope, atom_owner, atom_site, sphere_offset, displaced):
    point_cell = point_index(atom_owner, atom_site, sphere_offset)

    def operator(field):
        onsite = (potential[None, None, :] - band_energy[None, :, None]) * field
        return kinetic_part(field) + onsite + nonlocal_part(field, point_cell, beta_radial) + SHIFT * occupied_part(field, occupied)

    disp_cells = point_cell[displaced]
    values = occupied[:, disp_cells]
    first_proj = jnp.einsum("npk,k->pn", values, beta_radial, precision=HIGH)
    second_proj = jnp.einsum("npk,k->pn", values, beta_slope, precision=HIGH)
    update = STRENGTH * (first_proj[:, :, None] * beta_slope[None, None, :] + second_proj[:, :, None] * beta_radial[None, None, :])
    mixed = perturbation[:, None, :] * occupied[None, :, :]
    pert_ids = jnp.arange(NPERT, dtype=jnp.int32)[:, None, None]
    band_ids = jnp.arange(NOCC, dtype=jnp.int32)[None, :, None]
    mixed = mixed.at[pert_ids, band_ids, disp_cells[:, None, :]].add(update)
    rhs = -(mixed - occupied_part(mixed, occupied))

    solution = start_guess
    residual = rhs - operator(start_guess)
    direction = residual
    norm_now = jnp.sum(residual * residual, axis=2)
    for iteration in range(ITERS):
        image = operator(direction)
        alpha = norm_now / jnp.sum(direction * image, axis=2)
        solution = solution + alpha[:, :, None] * direction
        residual = residual - alpha[:, :, None] * image
        if iteration + 1 < ITERS:
            norm_next = jnp.sum(residual * residual, axis=2)
            direction = residual + (norm_next / norm_now)[:, :, None] * direction
            norm_now = norm_next
    return solution, residual
```

```python
import functools
import numpy as np
import jax
import jax.numpy as jnp
from jax import lax
from jax.experimental import pallas as pl
from jax.experimental.pallas import tpu as pltpu
from jax.sharding import PartitionSpec as P

NY = 16
NX = 16
PLANE = NY * NX
HALO = 6
RAD = 5

COEF = (
    -5369.0 / 1800.0,
    12.0 / 7.0,
    -15.0 / 56.0,
    10.0 / 189.0,
    -1.0 / 112.0,
    2.0 / 825.0,
    -1.0 / 1386.0,
)
KINETIC = 2.0
SHIFT = 20.0
STRENGTH = 10.0
HIGH = lax.Precision.HIGHEST


def plane_matrix():
    full = np.zeros((PLANE, PLANE), np.float64)
    for y in range(NY):
        for x in range(NX):
            at = y * NX + x
            full[at, at] += 3.0 * COEF[0]
            for d in range(1, 7):
                for s in (d, -d):
                    full[((y + s) % NY) * NX + x, at] += COEF[d]
                    full[y * NX + (x + s) % NX, at] += COEF[d]
    return (-KINETIC * full).astype(np.float32)


def fields_kernel(slabs, depth, radial, slope, offset, owner, site, displaced, out, pair, padded):
    atoms = out.shape[0]
    planes = slabs * depth
    points = offset.shape[1]
    slab = lax.axis_index("dom")
    rows = lax.broadcasted_iota(jnp.int32, (16, points), 0)
    along_z = rows == offset[0:1, :] + RAD
    in_plane = (offset[1:2, :] & (NY - 1)) * NX + (offset[2:3, :] & (NX - 1))
    hot = jnp.where(
        lax.broadcasted_iota(jnp.int32, (PLANE, points), 0) == in_plane, 1.0, 0.0
    ).astype(jnp.float32)
    left = jnp.concatenate(
        [jnp.where(along_z, radial[...], 0.0), jnp.where(along_z, slope[...], 0.0)], axis=0
    )
    template = lax.dot_general(
        left, hot, (((1,), (1,)), ((), ())), precision=HIGH, preferred_element_type=jnp.float32
    )
    padded[...] = jnp.zeros_like(padded)
    for which in range(2):
        part = template[16 * which : 16 * which + 16]
        padded[which, 0:16, :] = part
        padded[which, planes : planes + 16, :] = part
    column = lax.broadcasted_iota(jnp.int32, (8, PLANE), 1) & (NX - 1)

    def shifted(which, a):
        z = lax.rem(slab * depth + RAD + 2 * planes - owner[a] * depth - site[0, a], planes)
        x = site[2, a]
        turn = site[1, a] * NX + x
        start = pl.multiple_of(lax.div(z, 8) * 8, 8)
        block = pltpu.roll(padded[which, pl.ds(start, 16), :], lax.rem(16 - lax.rem(z, 8), 16), 0)[0:8]
        first = pltpu.roll(block, turn, 1)
        second = pltpu.roll(block, lax.rem(turn + PLANE - NX, PLANE), 1)
        return jnp.where(column >= x, first, second)

    for a in range(atoms):
        field = shifted(0, a)
        for z in range(depth):
            out[a : a + 1, z * PLANE : (z + 1) * PLANE] = field[z : z + 1]
    pair[...] = jnp.zeros_like(pair)
    for which in range(2):
        field = shifted(which, displaced[0])
        for z in range(depth):
            pair[which : which + 1, z * PLANE : (z + 1) * PLANE] = field[z : z + 1]


def atom_fields(slabs, cells, beta_radial, beta_slope, offset, owner, site, displaced):
    atoms = owner.shape[0]
    depth = cells // PLANE
    vmem = pl.BlockSpec(memory_space=pltpu.VMEM)
    smem = pl.BlockSpec(memory_space=pltpu.SMEM)
    return pl.pallas_call(
        functools.partial(fields_kernel, slabs, depth),
        out_shape=(
            jax.ShapeDtypeStruct((atoms, cells), jnp.float32),
            jax.ShapeDtypeStruct((8, cells), jnp.float32),
        ),
        in_specs=[vmem, vmem, vmem, smem, smem, smem],
        out_specs=(vmem, vmem),
        scratch_shapes=[pltpu.VMEM((2, slabs * depth + 16, PLANE), jnp.float32)],
        compiler_params=pltpu.CompilerParams(vmem_limit_bytes=16 * 1024 * 1024),
    )(beta_radial[None, :], beta_slope[None, :], offset, owner, site, displaced)


def times(a, b, dims):
    return lax.dot_general(a, b, (dims, ((), ())), precision=HIGH, preferred_element_type=jnp.float32)


def plain(occupied, start, potential, perturbation, energy, beta, pair, in_plane):
    slabs = lax.axis_size("dom")
    bands, cells = start.shape
    depth = cells // PLANE
    total = cells * slabs
    whole = lax.all_gather(occupied, "band", axis=0, tiled=True)
    every = whole.shape[0]
    up = [(i, (i + 1) % slabs) for i in range(slabs)]
    down = [(j, i) for i, j in up]

    def local_part(field):
        before = lax.ppermute(field, "dom", up)
        after = lax.ppermute(field, "dom", down)
        grid = jnp.concatenate([before, field, after], axis=1)
        image = times(field.reshape(bands * depth, PLANE), in_plane, ((1,), (0,))).reshape(bands, cells)
        for d in range(1, 7):
            low = (depth - d) * PLANE
            high = (depth + d) * PLANE
            image += (-KINETIC * COEF[d]) * (grid[:, low : low + cells] + grid[:, high : high + cells])
        return image + (potential - energy) * field

    def correlate(field):
        return jnp.concatenate(
            [times(field, whole, ((1,), (1,))), times(field, beta, ((1,), (1,)))], axis=1
        )

    def operator(field, total_correlation):
        return (
            local_part(field)
            + (SHIFT / total) * times(total_correlation[:, :every], whole, ((1,), (0,)))
            + STRENGTH * times(total_correlation[:, every:], beta, ((1,), (0,)))
        )

    def dot(u, v):
        return jnp.sum(u * v, axis=1, keepdims=True)

    shaped = perturbation * occupied
    first, on_atoms, own, of_all = lax.psum(
        (
            times(shaped - SHIFT * start, whole, ((1,), (1,))),
            times(start, beta, ((1,), (1,))),
            times(occupied, pair, ((1,), (1,))),
            times(pair, whole, ((1,), (1,))),
        ),
        "dom",
    )
    own_radial, own_slope = own[:, 0:1], own[:, 1:2]
    first = first + STRENGTH * (own_radial * of_all[1:2] + own_slope * of_all[0:1])
    residual = (
        times(first * (1.0 / total), whole, ((1,), (0,)))
        - STRENGTH * times(on_atoms, beta, ((1,), (0,)))
        - local_part(start)
        - shaped
        - STRENGTH * (own_radial * pair[1:2] + own_slope * pair[0:1])
    )
    correlation, norm = lax.psum((correlate(residual), dot(residual, residual)), "dom")
    image = operator(residual, correlation)
    correlation, curve = lax.psum((correlate(image), dot(residual, image)), "dom")
    alpha = norm / curve
    again = operator(image, correlation)
    later = residual - alpha * image
    later_image = image - alpha * again
    new, bend, cross = lax.psum((dot(later, later), dot(later, later_image), dot(later, image)), "dom")
    ratio = new / norm
    step = new / (bend + ratio * (2.0 * cross + ratio * curve))
    answer = start + alpha * residual + step * (later + ratio * residual)
    return answer, later - step * (later_image + ratio * image)


def local(
    occupied,
    start_guess,
    potential,
    perturbation,
    band_energy,
    beta_radial,
    beta_slope,
    atom_owner,
    atom_site,
    sphere_offset,
    displaced,
):
    slabs = lax.axis_size("dom")
    beta, pair = atom_fields(
        slabs,
        start_guess.shape[2],
        beta_radial,
        beta_slope,
        sphere_offset,
        atom_owner,
        atom_site,
        displaced,
    )
    in_plane = jnp.asarray(plane_matrix())
    answer, residual = plain(
        occupied,
        start_guess[0],
        potential[None, :],
        perturbation,
        band_energy[:, None],
        beta,
        pair,
        in_plane,
    )
    return answer[None], residual[None]


def solution(mesh):
    return jax.shard_map(
        local,
        mesh=mesh,
        in_specs=(
            P("band", "dom"),
            P(None, "band", "dom"),
            P("dom"),
            P(None, "dom"),
            P("band"),
            P(),
            P(),
            P(),
            P(),
            P(),
            P(),
        ),
        out_specs=(P(None, "band", "dom"), P(None, "band", "dom")),
        check_vma=False,
    )
```

```python
import functools
import numpy as np
import jax
import jax.numpy as jnp
from jax import lax
from jax.experimental import pallas as pl
from jax.experimental.pallas import tpu as pltpu
from jax.sharding import PartitionSpec as P

NY = 16
NX = 16
PLANE = NY * NX
HALO = 6
RAD = 5

COEF = (
    -5369.0 / 1800.0,
    12.0 / 7.0,
    -15.0 / 56.0,
    10.0 / 189.0,
    -1.0 / 112.0,
    2.0 / 825.0,
    -1.0 / 1386.0,
)
KINETIC = 2.0
SHIFT = 20.0
STRENGTH = 10.0
HIGH = lax.Precision.HIGHEST


def plane_matrix():
    full = np.zeros((PLANE, PLANE), np.float64)
    for y in range(NY):
        for x in range(NX):
            at = y * NX + x
            full[at, at] += 3.0 * COEF[0]
            for d in range(1, 7):
                for s in (d, -d):
                    full[((y + s) % NY) * NX + x, at] += COEF[d]
                    full[y * NX + (x + s) % NX, at] += COEF[d]
    return (-KINETIC * full).astype(np.float32)


def fields_kernel(slabs, depth, radial, slope, offset, owner, site, displaced, out, padded):
    atoms = owner.shape[0]
    planes = slabs * depth
    points = offset.shape[1]
    slab = lax.axis_index("dom")
    rows = lax.broadcasted_iota(jnp.int32, (16, points), 0)
    along_z = rows == offset[0:1, :] + RAD
    in_plane = (offset[1:2, :] & (NY - 1)) * NX + (offset[2:3, :] & (NX - 1))
    hot = jnp.where(
        lax.broadcasted_iota(jnp.int32, (PLANE, points), 0) == in_plane, 1.0, 0.0
    ).astype(jnp.float32)
    left = jnp.concatenate(
        [jnp.where(along_z, radial[...], 0.0), jnp.where(along_z, slope[...], 0.0)], axis=0
    )
    template = lax.dot_general(
        left, hot, (((1,), (1,)), ((), ())), precision=HIGH, preferred_element_type=jnp.float32
    )
    padded[...] = jnp.zeros_like(padded)
    for which in range(2):
        part = template[16 * which : 16 * which + 16]
        padded[which, 0:16, :] = part
        padded[which, planes : planes + 16, :] = part
    column = lax.broadcasted_iota(jnp.int32, (8, PLANE), 1) & (NX - 1)

    def shifted(which, a):
        z = lax.rem(slab * depth + RAD + 2 * planes - owner[a] * depth - site[0, a], planes)
        x = site[2, a]
        turn = site[1, a] * NX + x
        start = pl.multiple_of(lax.div(z, 8) * 8, 8)
        block = pltpu.roll(padded[which, pl.ds(start, 16), :], lax.rem(16 - lax.rem(z, 8), 16), 0)[0:8]
        first = pltpu.roll(block, turn, 1)
        second = pltpu.roll(block, lax.rem(turn + PLANE - NX, PLANE), 1)
        return jnp.where(column >= x, first, second)

    out[atoms:, :] = jnp.zeros((out.shape[0] - atoms, out.shape[1]), jnp.float32)
    for row in range(atoms + 2):
        field = shifted(0, row) if row < atoms else shifted(row - atoms, displaced[0])
        for z in range(depth):
            out[row : row + 1, z * PLANE : (z + 1) * PLANE] = field[z : z + 1]


def atom_fields(slabs, cells, beta_radial, beta_slope, offset, owner, site, displaced):
    atoms = owner.shape[0]
    depth = cells // PLANE
    vmem = pl.BlockSpec(memory_space=pltpu.VMEM)
    smem = pl.BlockSpec(memory_space=pltpu.SMEM)
    return pl.pallas_call(
        functools.partial(fields_kernel, slabs, depth),
        out_shape=jax.ShapeDtypeStruct((max(128, atoms + 16), cells), jnp.float32),
        in_specs=[vmem, vmem, vmem, smem, smem, smem],
        out_specs=vmem,
        scratch_shapes=[pltpu.VMEM((2, slabs * depth + 16, PLANE), jnp.float32)],
        compiler_params=pltpu.CompilerParams(vmem_limit_bytes=16 * 1024 * 1024),
    )(beta_radial[None, :], beta_slope[None, :], offset, owner, site, displaced)


def times(a, b, dims):
    return lax.dot_general(a, b, (dims, ((), ())), precision=HIGH, preferred_element_type=jnp.float32)


def plain(occupied, start, potential, perturbation, energy, beta, pair, in_plane):
    slabs = lax.axis_size("dom")
    bands, cells = start.shape
    depth = cells // PLANE
    total = cells * slabs
    whole = lax.all_gather(occupied, "band", axis=0, tiled=True)
    every = whole.shape[0]
    up = [(i, (i + 1) % slabs) for i in range(slabs)]
    down = [(j, i) for i, j in up]

    def local_part(field):
        before = lax.ppermute(field, "dom", up)
        after = lax.ppermute(field, "dom", down)
        grid = jnp.concatenate([before, field, after], axis=1)
        image = times(field.reshape(bands * depth, PLANE), in_plane, ((1,), (0,))).reshape(bands, cells)
        for d in range(1, 7):
            low = (depth - d) * PLANE
            high = (depth + d) * PLANE
            image += (-KINETIC * COEF[d]) * (grid[:, low : low + cells] + grid[:, high : high + cells])
        return image + (potential - energy) * field

    def correlate(field):
        return jnp.concatenate(
            [times(field, whole, ((1,), (1,))), times(field, beta, ((1,), (1,)))], axis=1
        )

    def operator(field, total_correlation):
        return (
            local_part(field)
            + (SHIFT / total) * times(total_correlation[:, :every], whole, ((1,), (0,)))
            + STRENGTH * times(total_correlation[:, every:], beta, ((1,), (0,)))
        )

    def dot(u, v):
        return jnp.sum(u * v, axis=1, keepdims=True)

    shaped = perturbation * occupied
    first, on_atoms, own, of_all = lax.psum(
        (
            times(shaped - SHIFT * start, whole, ((1,), (1,))),
            times(start, beta, ((1,), (1,))),
            times(occupied, pair, ((1,), (1,))),
            times(pair, whole, ((1,), (1,))),
        ),
        "dom",
    )
    own_radial, own_slope = own[:, 0:1], own[:, 1:2]
    first = first + STRENGTH * (own_radial * of_all[1:2] + own_slope * of_all[0:1])
    residual = (
        times(first * (1.0 / total), whole, ((1,), (0,)))
        - STRENGTH * times(on_atoms, beta, ((1,), (0,)))
        - local_part(start)
        - shaped
        - STRENGTH * (own_radial * pair[1:2] + own_slope * pair[0:1])
    )
    correlation, norm = lax.psum((correlate(residual), dot(residual, residual)), "dom")
    image = operator(residual, correlation)
    correlation, curve = lax.psum((correlate(image), dot(residual, image)), "dom")
    alpha = norm / curve
    again = operator(image, correlation)
    later = residual - alpha * image
    later_image = image - alpha * again
    new, bend, cross = lax.psum((dot(later, later), dot(later, later_image), dot(later, image)), "dom")
    ratio = new / norm
    step = new / (bend + ratio * (2.0 * cross + ratio * curve))
    answer = start + alpha * residual + step * (later + ratio * residual)
    return answer, later - step * (later_image + ratio * image)


NT = (((1,), (1,)), ((), ()))
NN = (((1,), (0,)), ((), ()))
MESH = pl.DeviceIdType.MESH


def parts_of(x):
    high = x.astype(jnp.bfloat16)
    return high, (x - high.astype(jnp.float32)).astype(jnp.bfloat16)


def product(a, b, dims):
    def one(u, v):
        return lax.dot_general(u, v, dims, preferred_element_type=jnp.float32)

    return one(a[0], b[0]) + (one(a[0], b[1]) + one(a[1], b[0]))


def fused_kernel(
    atoms,
    slabs,
    occ,
    start,
    pot,
    pert,
    energy,
    fields,
    plane_high,
    plane_low,
    answer,
    residual,
    whole,
    w_high,
    w_low,
    f_high,
    f_low,
    before,
    after,
    r0,
    w0,
    image,
    part,
    pieces,
    summed,
    totals,
    rows_part,
    rows_in,
    last_part,
    last_in,
    band_send,
    band_recv,
    halo_send,
    halo_recv,
    sum_send,
    sum_recv,
    all_send,
    all_recv,
    rows_send,
    rows_recv,
    last_send,
    last_recv,
):
    bands, cells = occ.shape
    every = 4 * bands
    total = cells * slabs
    band = lax.axis_index("band")
    slab = lax.axis_index("dom")
    sibling = band + 1 - 2 * (band % 2)
    across = (band + 2) % 4
    barrier = pltpu.get_barrier_semaphore()
    pl.semaphore_signal(barrier, inc=1, device_id={"band": sibling}, device_id_type=MESH)
    pl.semaphore_signal(barrier, inc=1, device_id={"band": across}, device_id_type=MESH)
    peers = [(slab + k) % slabs for k in range(slabs)]
    for k in range(1, slabs):
        pl.semaphore_signal(barrier, inc=1, device_id={"dom": peers[k]}, device_id_type=MESH)
    pl.semaphore_wait(barrier, slabs + 1)

    pending = []

    def send(src, dst, send_sem, recv_sem, device):
        copy = pltpu.make_async_remote_copy(
            src_ref=src,
            dst_ref=dst,
            send_sem=send_sem,
            recv_sem=recv_sem,
            device_id=device,
            device_id_type=MESH,
        )
        copy.start()
        pending.append(copy)
        return copy

    def exchange_faces(turn, field):
        return (
            send(field, before.at[turn], halo_send.at[turn, 0], halo_recv.at[turn, 0], {"dom": peers[1]}),
            send(
                field, after.at[turn], halo_send.at[turn, 1], halo_recv.at[turn, 1], {"dom": peers[slabs - 1]}
            ),
        )

    half = bands // 2
    crossing = [
        send(
            occ.at[pl.ds(c * half, half)],
            whole.at[1, pl.ds(c * half, half)],
            band_send.at[c],
            band_recv.at[c],
            {"band": across},
        )
        for c in range(2)
    ]
    to_sibling = send(occ, whole.at[0], band_send.at[2], band_recv.at[2], {"band": sibling})
    faces = exchange_faces(0, start)

    def hold(row, block):
        high, low = parts_of(block)
        w_high[row : row + block.shape[0], :] = high
        w_low[row : row + block.shape[0], :] = low

    def hold_field(block):
        high, low = parts_of(block)
        f_high[...] = high
        f_low[...] = low

    def plane_image(field):
        for z in range(HALO):
            cut = slice(z * PLANE, (z + 1) * PLANE)
            image[:, cut] = product(
                (f_high[:, cut], f_low[:, cut]), (plane_high[...], plane_low[...]), NN
            ) + (pot[:, cut] - energy[...]) * field[:, cut]

    def across_planes(turn, field):
        def group(i, carry):
            rows = pl.ds(pl.multiple_of(i * 8, 8), 8)
            grid = [
                ref[rows, z * PLANE : (z + 1) * PLANE]
                for ref in (before.at[turn], field, after.at[turn])
                for z in range(HALO)
            ]
            for z in range(HALO):
                cut = slice(z * PLANE, (z + 1) * PLANE)
                value = image[rows, cut]
                for d in range(1, 7):
                    value += (-KINETIC * COEF[d]) * (grid[HALO + z - d] + grid[HALO + z + d])
                image[rows, cut] = value
            return carry

        lax.fori_loop(0, bands // 8, group, 0)

    def start_sum(turn):
        return [
            send(
                part.at[turn, pl.ds(pl.multiple_of(peers[k] * 8, 8), 8)],
                pieces.at[turn, k],
                sum_send.at[turn, k],
                sum_recv.at[turn, k],
                {"dom": peers[k]},
            )
            for k in range(1, slabs)
        ]

    def share_sum(turn, copies):
        mine = pl.ds(pl.multiple_of(slab * 8, 8), 8)
        value = part[turn, mine, :]
        for k in range(1, slabs):
            copies[k - 1].wait_recv()
            value += pieces[turn, k]
        summed[turn] = value
        shared = [
            send(
                summed.at[turn],
                totals.at[turn, mine],
                all_send.at[turn, k],
                all_recv.at[turn, k],
                {"dom": peers[k]},
            )
            for k in range(1, slabs)
        ]
        totals[turn, mine, :] = value
        return shared

    def finish_sum(shared):
        for copy in shared:
            copy.wait_recv()

    lane = lax.broadcasted_iota(jnp.int32, (bands, 128), 1)

    def correlate(rows):
        return product((f_high[...], f_low[...]), (w_high[rows, :], w_low[rows, :]), NT)

    def back(coefficients):
        return product(parts_of(coefficients), (w_high[...], w_low[...]), NN)

    hold(0, occ[...])
    hold(every, fields[...])
    hold_field(start[...])
    plane_image(start)
    ends = slice(every, every + 128)
    on_start = correlate(ends)
    on_own = product(
        (w_high[0:bands, :], w_low[0:bands, :]), (w_high[ends, :], w_low[ends, :]), NT
    )
    part[0, :, every:] = jnp.where(lane < atoms, on_start, on_own)
    shaped = pert[...] * occ[...]
    hold_field(shaped - SHIFT * start[...])
    to_sibling.wait_recv()
    hold(bands, whole[0])
    part[0, :, 0 : 2 * bands] = correlate(slice(0, 2 * bands))
    passed = []
    for c in range(2):
        crossing[c].wait_recv()
        passed.append(
            send(
                whole.at[1, pl.ds(c * half, half)],
                whole.at[2, pl.ds(c * half, half)],
                band_send.at[3 + c],
                band_recv.at[3 + c],
                {"band": sibling},
            )
        )
    hold(2 * bands, whole[1])
    for copy in passed:
        copy.wait_recv()
    hold(3 * bands, whole[2])
    part[0, :, 2 * bands : every] = correlate(slice(2 * bands, every))
    copies = start_sum(0)
    pair = slice(every + atoms, every + atoms + 16)
    rows_part[...] = product(
        (w_high[pair, :], w_low[pair, :]), (w_high[0:every, :], w_low[0:every, :]), NT
    )[0:8]
    row_copies = [
        send(rows_part, rows_in.at[k], rows_send.at[k], rows_recv.at[k], {"dom": peers[k]})
        for k in range(1, slabs)
    ]
    shared = share_sum(0, copies)
    for copy in faces:
        copy.wait_recv()
    across_planes(0, start)
    of_all = rows_part[...]
    for k in range(1, slabs):
        row_copies[k - 1].wait_recv()
        of_all += rows_in[k]
    finish_sum(shared)
    last = totals[0, :, every:]
    own_radial, own_slope = last[:, atoms : atoms + 1], last[:, atoms + 1 : atoms + 2]
    first = totals[0, :, 0:every] + STRENGTH * (own_radial * of_all[1:2] + own_slope * of_all[0:1])
    ends_part = jnp.where(
        lane < atoms,
        last,
        jnp.where(lane == atoms, own_slope, jnp.where(lane == atoms + 1, own_radial, 0.0)),
    )
    r0[...] = (
        back(jnp.concatenate([first * (1.0 / total), -STRENGTH * ends_part], axis=1))
        - image[...]
        - pert[...] * occ[...]
    )

    def apply(turn, field, scalar):
        faces = exchange_faces(turn, field)
        hold_field(field[...])
        part[turn, :, 0:every] = correlate(slice(0, every))
        part[turn, :, every:] = jnp.where(lane == atoms, scalar, correlate(ends))
        copies = start_sum(turn)
        plane_image(field)
        shared = share_sum(turn, copies)
        for copy in faces:
            copy.wait_recv()
        across_planes(turn, field)
        finish_sum(shared)
        last = totals[turn, :, every:]
        coefficients = jnp.concatenate(
            [
                totals[turn, :, 0:every] * (SHIFT / total),
                jnp.where(lane < atoms, STRENGTH * last, 0.0),
            ],
            axis=1,
        )
        image[...] += back(coefficients)
        return last[:, atoms : atoms + 1]

    def dot(u, v):
        return jnp.sum(u * v, axis=1, keepdims=True)

    norm = apply(1, r0, dot(r0[...], r0[...]))
    w0[...] = image[...]
    curve = apply(2, w0, dot(r0[...], w0[...]))
    alpha = norm / curve
    later = r0[...] - alpha * w0[...]
    later_image = w0[...] - alpha * image[...]
    residual[0] = later
    image[...] = later_image
    three = jnp.where(
        lane == 0,
        dot(later, later),
        jnp.where(
            lane == 1, dot(later, later_image), jnp.where(lane == 2, dot(later, w0[...]), 0.0)
        ),
    )
    eye = jnp.where(
        lax.broadcasted_iota(jnp.int32, (128, 128), 0)
        == lax.broadcasted_iota(jnp.int32, (128, 128), 1),
        1.0,
        0.0,
    ).astype(jnp.float32)
    three = jnp.concatenate([three, jnp.zeros((128 - bands, 128), jnp.float32)], axis=0)
    last_part[...] = lax.dot_general(
        eye[0:8], three, NT, precision=HIGH, preferred_element_type=jnp.float32
    )
    last_copies = [
        send(last_part, last_in.at[k], last_send.at[k], last_recv.at[k], {"dom": peers[k]})
        for k in range(1, slabs)
    ]
    value = last_part[...]
    for k in range(1, slabs):
        last_copies[k - 1].wait_recv()
        value += last_in[k]
    three = lax.dot_general(
        eye[0:bands], value, NT, precision=HIGH, preferred_element_type=jnp.float32
    )
    new, bend, cross = three[:, 0:1], three[:, 1:2], three[:, 2:3]
    ratio = new / norm
    step = new / (bend + ratio * (2.0 * cross + ratio * curve))
    later = residual[0]
    answer[0] = start[...] + alpha * r0[...] + step * (later + ratio * r0[...])
    residual[0] = later - step * (image[...] + ratio * w0[...])
    for copy in pending:
        copy.wait_send()


def fused(atoms, occupied, start_guess, potential, perturbation, energy, fields, in_plane):
    slabs = lax.axis_size("dom")
    bands, cells = occupied.shape
    every = 4 * bands
    rows = every + 128
    plane_high = in_plane.astype(jnp.bfloat16)
    plane_low = (in_plane - plane_high.astype(np.float32)).astype(jnp.bfloat16)
    f32, bf16 = jnp.float32, jnp.bfloat16
    vmem = pl.BlockSpec(memory_space=pltpu.VMEM)
    out = jax.ShapeDtypeStruct((1, bands, cells), f32)
    dma = pltpu.SemaphoreType.DMA
    field = pltpu.VMEM((bands, cells), f32)
    return pl.pallas_call(
        functools.partial(fused_kernel, atoms, slabs),
        out_shape=(out, out),
        in_specs=[vmem] * 8,
        out_specs=(vmem, vmem),
        scratch_shapes=[
            pltpu.VMEM((3, bands, cells), f32),
            pltpu.VMEM((rows, cells), bf16),
            pltpu.VMEM((rows, cells), bf16),
            pltpu.VMEM((bands, cells), bf16),
            pltpu.VMEM((bands, cells), bf16),
            pltpu.VMEM((3, bands, cells), f32),
            pltpu.VMEM((3, bands, cells), f32),
            field,
            field,
            field,
            pltpu.VMEM((3, bands, rows), f32),
            pltpu.VMEM((3, slabs, 8, rows), f32),
            pltpu.VMEM((3, 8, rows), f32),
            pltpu.VMEM((3, bands, rows), f32),
            pltpu.VMEM((8, every), f32),
            pltpu.VMEM((slabs, 8, every), f32),
            pltpu.VMEM((8, 128), f32),
            pltpu.VMEM((slabs, 8, 128), f32),
            dma((5,)),
            dma((5,)),
            dma((3, 2)),
            dma((3, 2)),
            dma((3, slabs)),
            dma((3, slabs)),
            dma((3, slabs)),
            dma((3, slabs)),
            dma((slabs,)),
            dma((slabs,)),
            dma((slabs,)),
            dma((slabs,)),
        ],
        compiler_params=pltpu.CompilerParams(
            collective_id=0, has_side_effects=True, vmem_limit_bytes=40 * 1024 * 1024
        ),
    )(
        occupied,
        start_guess[0],
        potential,
        perturbation,
        energy,
        fields,
        jnp.asarray(plane_high),
        jnp.asarray(plane_low),
    )


def local(
    occupied,
    start_guess,
    potential,
    perturbation,
    band_energy,
    beta_radial,
    beta_slope,
    atom_owner,
    atom_site,
    sphere_offset,
    displaced,
):
    slabs = lax.axis_size("dom")
    bands, cells = start_guess.shape[1:]
    atoms = atom_owner.shape[0]
    fields = atom_fields(
        slabs, cells, beta_radial, beta_slope, sphere_offset, atom_owner, atom_site, displaced
    )
    in_plane = plane_matrix()
    fits = bands == 8 * slabs and lax.axis_size("band") == 4 and atoms % 16 == 0 and atoms <= 112
    if fits and cells == HALO * PLANE:
        return fused(
            atoms,
            occupied,
            start_guess,
            potential[None, :],
            perturbation,
            band_energy[:, None],
            fields,
            in_plane,
        )
    answer, residual = plain(
        occupied,
        start_guess[0],
        potential[None, :],
        perturbation,
        band_energy[:, None],
        fields[:atoms],
        fields[atoms : atoms + 8],
        jnp.asarray(in_plane),
    )
    return answer[None], residual[None]


def solution(mesh):
    return jax.shard_map(
        local,
        mesh=mesh,
        in_specs=(
            P("band", "dom"),
            P(None, "band", "dom"),
            P("dom"),
            P(None, "dom"),
            P("band"),
            P(),
            P(),
            P(),
            P(),
            P(),
            P(),
        ),
        out_specs=(P(None, "band", "dom"), P(None, "band", "dom")),
        check_vma=False,
    )
```

```python
import functools
import numpy as np
import jax
import jax.numpy as jnp
from jax import lax
from jax.experimental import pallas as pl
from jax.experimental.pallas import tpu as pltpu
from jax.sharding import PartitionSpec as P

NY = 16
NX = 16
PLANE = NY * NX
HALO = 6
CHUNKS = 4
RAD = 5

COEF = (
    -5369.0 / 1800.0,
    12.0 / 7.0,
    -15.0 / 56.0,
    10.0 / 189.0,
    -1.0 / 112.0,
    2.0 / 825.0,
    -1.0 / 1386.0,
)
KINETIC = 2.0
SHIFT = 20.0
STRENGTH = 10.0
HIGH = lax.Precision.HIGHEST


def plane_matrix():
    full = np.zeros((PLANE, PLANE), np.float64)
    for y in range(NY):
        for x in range(NX):
            at = y * NX + x
            full[at, at] += 3.0 * COEF[0]
            for d in range(1, 7):
                for s in (d, -d):
                    full[((y + s) % NY) * NX + x, at] += COEF[d]
                    full[y * NX + (x + s) % NX, at] += COEF[d]
    return (-KINETIC * full).astype(np.float32)


def fields_kernel(slabs, depth, radial, slope, offset, owner, site, displaced, out, padded):
    atoms = owner.shape[0]
    planes = slabs * depth
    points = offset.shape[1]
    slab = lax.axis_index("dom")
    rows = lax.broadcasted_iota(jnp.int32, (16, points), 0)
    along_z = rows == offset[0:1, :] + RAD
    in_plane = (offset[1:2, :] & (NY - 1)) * NX + (offset[2:3, :] & (NX - 1))
    hot = jnp.where(
        lax.broadcasted_iota(jnp.int32, (PLANE, points), 0) == in_plane, 1.0, 0.0
    ).astype(jnp.float32)
    left = jnp.concatenate(
        [jnp.where(along_z, radial[...], 0.0), jnp.where(along_z, slope[...], 0.0)], axis=0
    )
    template = lax.dot_general(
        left, hot, (((1,), (1,)), ((), ())), precision=HIGH, preferred_element_type=jnp.float32
    )
    padded[...] = jnp.zeros_like(padded)
    for which in range(2):
        part = template[16 * which : 16 * which + 16]
        padded[which, 0:16, :] = part
        padded[which, planes : planes + 16, :] = part
    column = lax.broadcasted_iota(jnp.int32, (8, PLANE), 1) & (NX - 1)

    def shifted(which, a):
        z = lax.rem(slab * depth + RAD + 2 * planes - owner[a] * depth - site[0, a], planes)
        x = site[2, a]
        turn = site[1, a] * NX + x
        start = pl.multiple_of(lax.div(z, 8) * 8, 8)
        block = pltpu.roll(padded[which, pl.ds(start, 16), :], lax.rem(16 - lax.rem(z, 8), 16), 0)[0:8]
        first = pltpu.roll(block, turn, 1)
        second = pltpu.roll(block, lax.rem(turn + PLANE - NX, PLANE), 1)
        return jnp.where(column >= x, first, second)

    out[atoms:, :] = jnp.zeros((out.shape[0] - atoms, out.shape[1]), jnp.float32)
    for row in range(atoms + 2):
        field = shifted(0, row) if row < atoms else shifted(row - atoms, displaced[0])
        for z in range(depth):
            out[row : row + 1, z * PLANE : (z + 1) * PLANE] = field[z : z + 1]


def atom_fields(slabs, cells, beta_radial, beta_slope, offset, owner, site, displaced):
    atoms = owner.shape[0]
    depth = cells // PLANE
    vmem = pl.BlockSpec(memory_space=pltpu.VMEM)
    smem = pl.BlockSpec(memory_space=pltpu.SMEM)
    return pl.pallas_call(
        functools.partial(fields_kernel, slabs, depth),
        out_shape=jax.ShapeDtypeStruct((max(128, atoms + 16), cells), jnp.float32),
        in_specs=[vmem, vmem, vmem, smem, smem, smem],
        out_specs=vmem,
        scratch_shapes=[pltpu.VMEM((2, slabs * depth + 16, PLANE), jnp.float32)],
        compiler_params=pltpu.CompilerParams(vmem_limit_bytes=16 * 1024 * 1024),
    )(beta_radial[None, :], beta_slope[None, :], offset, owner, site, displaced)


def times(a, b, dims):
    return lax.dot_general(a, b, (dims, ((), ())), precision=HIGH, preferred_element_type=jnp.float32)


def plain(occupied, start, potential, perturbation, energy, beta, pair, in_plane):
    slabs = lax.axis_size("dom")
    bands, cells = start.shape
    depth = cells // PLANE
    total = cells * slabs
    whole = lax.all_gather(occupied, "band", axis=0, tiled=True)
    every = whole.shape[0]
    up = [(i, (i + 1) % slabs) for i in range(slabs)]
    down = [(j, i) for i, j in up]

    def local_part(field):
        before = lax.ppermute(field, "dom", up)
        after = lax.ppermute(field, "dom", down)
        grid = jnp.concatenate([before, field, after], axis=1)
        image = times(field.reshape(bands * depth, PLANE), in_plane, ((1,), (0,))).reshape(bands, cells)
        for d in range(1, 7):
            low = (depth - d) * PLANE
            high = (depth + d) * PLANE
            image += (-KINETIC * COEF[d]) * (grid[:, low : low + cells] + grid[:, high : high + cells])
        return image + (potential - energy) * field

    def correlate(field):
        return jnp.concatenate(
            [times(field, whole, ((1,), (1,))), times(field, beta, ((1,), (1,)))], axis=1
        )

    def operator(field, total_correlation):
        return (
            local_part(field)
            + (SHIFT / total) * times(total_correlation[:, :every], whole, ((1,), (0,)))
            + STRENGTH * times(total_correlation[:, every:], beta, ((1,), (0,)))
        )

    def dot(u, v):
        return jnp.sum(u * v, axis=1, keepdims=True)

    shaped = perturbation * occupied
    first, on_atoms, own, of_all = lax.psum(
        (
            times(shaped - SHIFT * start, whole, ((1,), (1,))),
            times(start, beta, ((1,), (1,))),
            times(occupied, pair, ((1,), (1,))),
            times(pair, whole, ((1,), (1,))),
        ),
        "dom",
    )
    own_radial, own_slope = own[:, 0:1], own[:, 1:2]
    first = first + STRENGTH * (own_radial * of_all[1:2] + own_slope * of_all[0:1])
    residual = (
        times(first * (1.0 / total), whole, ((1,), (0,)))
        - STRENGTH * times(on_atoms, beta, ((1,), (0,)))
        - local_part(start)
        - shaped
        - STRENGTH * (own_radial * pair[1:2] + own_slope * pair[0:1])
    )
    correlation, norm = lax.psum((correlate(residual), dot(residual, residual)), "dom")
    image = operator(residual, correlation)
    correlation, curve = lax.psum((correlate(image), dot(residual, image)), "dom")
    alpha = norm / curve
    again = operator(image, correlation)
    later = residual - alpha * image
    later_image = image - alpha * again
    new, bend, cross = lax.psum((dot(later, later), dot(later, later_image), dot(later, image)), "dom")
    ratio = new / norm
    step = new / (bend + ratio * (2.0 * cross + ratio * curve))
    answer = start + alpha * residual + step * (later + ratio * residual)
    return answer, later - step * (later_image + ratio * image)


NT = (((1,), (1,)), ((), ()))
NN = (((1,), (0,)), ((), ()))
MESH = pl.DeviceIdType.MESH


def parts_of(x):
    high = x.astype(jnp.bfloat16)
    return high, (x - high.astype(jnp.float32)).astype(jnp.bfloat16)


def product(a, b, dims):
    def one(u, v):
        return lax.dot_general(u, v, dims, preferred_element_type=jnp.float32)

    return one(a[0], b[0]) + (one(a[0], b[1]) + one(a[1], b[0]))


def fused_kernel(
    atoms,
    slabs,
    occ,
    start,
    pot,
    pert,
    energy,
    fields,
    plane_high,
    plane_low,
    answer,
    residual,
    whole,
    w_high,
    w_low,
    f_high,
    f_low,
    faces,
    r0,
    w0,
    image,
    part,
    pieces,
    summed,
    totals,
    rows_part,
    rows_in,
    last_part,
    last_in,
    band_send,
    band_recv,
    face_send,
    face_recv,
    hand_send,
    hand_recv,
    sum_send,
    sum_recv,
    all_send,
    all_recv,
    rows_send,
    rows_recv,
    last_send,
    last_recv,
):
    bands, cells = occ.shape
    every = 4 * bands
    total = cells * slabs
    band = lax.axis_index("band")
    slab = lax.axis_index("dom")
    sibling = band + 1 - 2 * (band % 2)
    across = (band + 2) % 4
    barrier = pltpu.get_barrier_semaphore()
    pl.semaphore_signal(barrier, inc=1, device_id={"band": sibling}, device_id_type=MESH)
    pl.semaphore_signal(barrier, inc=1, device_id={"band": across}, device_id_type=MESH)
    peers = [(slab + k) % slabs for k in range(slabs)]
    for k in range(1, slabs):
        pl.semaphore_signal(barrier, inc=1, device_id={"dom": peers[k]}, device_id_type=MESH)
    pl.semaphore_wait(barrier, slabs + 1)

    pending = []

    def send(src, dst, send_sem, recv_sem, device):
        copy = pltpu.make_async_remote_copy(
            src_ref=src,
            dst_ref=dst,
            send_sem=send_sem,
            recv_sem=recv_sem,
            device_id=device,
            device_id_type=MESH,
        )
        copy.start()
        pending.append(copy)
        return copy

    chunk = bands // CHUNKS
    side = slab % 2
    beside = slab + 1 - 2 * side
    beyond = (slab + slabs + 2 - 4 * side) % slabs

    def send_face(turn, field):
        return [
            send(
                field.at[pl.ds(c * chunk, chunk)],
                faces.at[turn, side, pl.ds(c * chunk, chunk)],
                face_send.at[turn, c],
                face_recv.at[turn, c],
                {"dom": beside},
            )
            for c in range(CHUNKS)
        ]

    def hand_on(turn, copies, c):
        copies[c].wait_recv()
        block = faces.at[turn, 1 - side, pl.ds(c * chunk, chunk)]
        copies.append(
            send(
                block,
                faces.at[turn, side, pl.ds(c * chunk, chunk)],
                hand_send.at[turn, c],
                hand_recv.at[turn, c],
                {"dom": beyond},
            )
        )

    half = bands // 2
    crossing = [
        send(
            occ.at[pl.ds(c * half, half)],
            whole.at[1, pl.ds(c * half, half)],
            band_send.at[c],
            band_recv.at[c],
            {"band": across},
        )
        for c in range(2)
    ]
    to_sibling = send(occ, whole.at[0], band_send.at[2], band_recv.at[2], {"band": sibling})
    moving = send_face(0, start)

    def hold(row, block):
        high, low = parts_of(block)
        w_high[row : row + block.shape[0], :] = high
        w_low[row : row + block.shape[0], :] = low

    def hold_field(block):
        high, low = parts_of(block)
        f_high[...] = high
        f_low[...] = low

    def plane_image(field, planes):
        for z in planes:
            cut = slice(z * PLANE, (z + 1) * PLANE)
            image[:, cut] = product(
                (f_high[:, cut], f_low[:, cut]), (plane_high[...], plane_low[...]), NN
            ) + (pot[:, cut] - energy[...]) * field[:, cut]

    def across_planes(turn, field, copies, c):
        copies[CHUNKS + c].wait_recv()

        def group(i, carry):
            rows = pl.ds(pl.multiple_of(i * 8, 8), 8)
            grid = [
                ref[rows, z * PLANE : (z + 1) * PLANE]
                for ref in (faces.at[turn, 0], field, faces.at[turn, 1])
                for z in range(HALO)
            ]
            for z in range(HALO):
                cut = slice(z * PLANE, (z + 1) * PLANE)
                value = image[rows, cut]
                for d in range(1, 7):
                    value += (-KINETIC * COEF[d]) * (grid[HALO + z - d] + grid[HALO + z + d])
                image[rows, cut] = value
            return carry

        lax.fori_loop(c * chunk // 8, (c + 1) * chunk // 8, group, 0)

    def start_sum(turn):
        return [
            send(
                part.at[turn, pl.ds(pl.multiple_of(peers[k] * 8, 8), 8)],
                pieces.at[turn, k],
                sum_send.at[turn, k],
                sum_recv.at[turn, k],
                {"dom": peers[k]},
            )
            for k in range(1, slabs)
        ]

    def share_sum(turn, copies):
        mine = pl.ds(pl.multiple_of(slab * 8, 8), 8)
        value = part[turn, mine, :]
        for k in range(1, slabs):
            copies[k - 1].wait_recv()
            value += pieces[turn, k]
        summed[turn] = value
        shared = [
            send(
                summed.at[turn],
                totals.at[turn, mine],
                all_send.at[turn, k],
                all_recv.at[turn, k],
                {"dom": peers[k]},
            )
            for k in range(1, slabs)
        ]
        totals[turn, mine, :] = value
        return shared

    def finish_sum(shared):
        for copy in shared:
            copy.wait_recv()

    lane = lax.broadcasted_iota(jnp.int32, (bands, 128), 1)

    def correlate(rows):
        return product((f_high[...], f_low[...]), (w_high[rows, :], w_low[rows, :]), NT)

    def back(coefficients):
        return product(parts_of(coefficients), (w_high[...], w_low[...]), NN)

    hold(0, occ[...])
    hold(every, fields[...])
    hold_field(start[...])
    plane_image(start, range(HALO))
    hand_on(0, moving, 0)
    ends = slice(every, every + 128)
    on_start = correlate(ends)
    on_own = product(
        (w_high[0:bands, :], w_low[0:bands, :]), (w_high[ends, :], w_low[ends, :]), NT
    )
    part[0, :, every:] = jnp.where(lane < atoms, on_start, on_own)
    hand_on(0, moving, 1)
    shaped = pert[...] * occ[...]
    hold_field(shaped - SHIFT * start[...])
    to_sibling.wait_recv()
    hold(bands, whole[0])
    part[0, :, 0 : 2 * bands] = correlate(slice(0, 2 * bands))
    passed = []
    for c in range(2):
        hand_on(0, moving, 2 + c)
        crossing[c].wait_recv()
        passed.append(
            send(
                whole.at[1, pl.ds(c * half, half)],
                whole.at[2, pl.ds(c * half, half)],
                band_send.at[3 + c],
                band_recv.at[3 + c],
                {"band": sibling},
            )
        )
    hold(2 * bands, whole[1])
    for copy in passed:
        copy.wait_recv()
    hold(3 * bands, whole[2])
    part[0, :, 2 * bands : every] = correlate(slice(2 * bands, every))
    copies = start_sum(0)
    pair = slice(every + atoms, every + atoms + 16)
    rows_part[...] = product(
        (w_high[pair, :], w_low[pair, :]), (w_high[0:every, :], w_low[0:every, :]), NT
    )[0:8]
    row_copies = [
        send(rows_part, rows_in.at[k], rows_send.at[k], rows_recv.at[k], {"dom": peers[k]})
        for k in range(1, slabs)
    ]
    shared = share_sum(0, copies)
    for c in range(CHUNKS):
        across_planes(0, start, moving, c)
    of_all = rows_part[...]
    for k in range(1, slabs):
        row_copies[k - 1].wait_recv()
        of_all += rows_in[k]
    finish_sum(shared)
    last = totals[0, :, every:]
    own_radial, own_slope = last[:, atoms : atoms + 1], last[:, atoms + 1 : atoms + 2]
    first = totals[0, :, 0:every] + STRENGTH * (own_radial * of_all[1:2] + own_slope * of_all[0:1])
    ends_part = jnp.where(
        lane < atoms,
        last,
        jnp.where(lane == atoms, own_slope, jnp.where(lane == atoms + 1, own_radial, 0.0)),
    )
    r0[...] = (
        back(jnp.concatenate([first * (1.0 / total), -STRENGTH * ends_part], axis=1))
        - image[...]
        - pert[...] * occ[...]
    )

    def apply(turn, field, scalar):
        moving = send_face(turn, field)
        hold_field(field[...])
        part[turn, :, every:] = jnp.where(lane == atoms, scalar, correlate(ends))
        hand_on(turn, moving, 0)
        part[turn, :, 0 : every // 2] = correlate(slice(0, every // 2))
        hand_on(turn, moving, 1)
        part[turn, :, every // 2 : every] = correlate(slice(every // 2, every))
        copies = start_sum(turn)
        hand_on(turn, moving, 2)
        plane_image(field, range(0, HALO // 2))
        hand_on(turn, moving, 3)
        plane_image(field, range(HALO // 2, HALO))
        shared = share_sum(turn, copies)
        for c in range(CHUNKS):
            across_planes(turn, field, moving, c)
        finish_sum(shared)
        last = totals[turn, :, every:]
        coefficients = jnp.concatenate(
            [
                totals[turn, :, 0:every] * (SHIFT / total),
                jnp.where(lane < atoms, STRENGTH * last, 0.0),
            ],
            axis=1,
        )
        image[...] += back(coefficients)
        return last[:, atoms : atoms + 1]

    def dot(u, v):
        return jnp.sum(u * v, axis=1, keepdims=True)

    norm = apply(1, r0, dot(r0[...], r0[...]))
    w0[...] = image[...]
    curve = apply(2, w0, dot(r0[...], w0[...]))
    alpha = norm / curve
    later = r0[...] - alpha * w0[...]
    later_image = w0[...] - alpha * image[...]
    residual[0] = later
    image[...] = later_image
    three = jnp.where(
        lane == 0,
        dot(later, later),
        jnp.where(
            lane == 1, dot(later, later_image), jnp.where(lane == 2, dot(later, w0[...]), 0.0)
        ),
    )
    eye = jnp.where(
        lax.broadcasted_iota(jnp.int32, (128, 128), 0)
        == lax.broadcasted_iota(jnp.int32, (128, 128), 1),
        1.0,
        0.0,
    ).astype(jnp.float32)
    three = jnp.concatenate([three, jnp.zeros((128 - bands, 128), jnp.float32)], axis=0)
    last_part[...] = lax.dot_general(
        eye[0:8], three, NT, precision=HIGH, preferred_element_type=jnp.float32
    )
    last_copies = [
        send(last_part, last_in.at[k], last_send.at[k], last_recv.at[k], {"dom": peers[k]})
        for k in range(1, slabs)
    ]
    value = last_part[...]
    for k in range(1, slabs):
        last_copies[k - 1].wait_recv()
        value += last_in[k]
    three = lax.dot_general(
        eye[0:bands], value, NT, precision=HIGH, preferred_element_type=jnp.float32
    )
    new, bend, cross = three[:, 0:1], three[:, 1:2], three[:, 2:3]
    ratio = new / norm
    step = new / (bend + ratio * (2.0 * cross + ratio * curve))
    later = residual[0]
    answer[0] = start[...] + alpha * r0[...] + step * (later + ratio * r0[...])
    residual[0] = later - step * (image[...] + ratio * w0[...])
    for copy in pending:
        copy.wait_send()


def fused(atoms, occupied, start_guess, potential, perturbation, energy, fields, in_plane):
    slabs = lax.axis_size("dom")
    bands, cells = occupied.shape
    every = 4 * bands
    rows = every + 128
    plane_high = in_plane.astype(jnp.bfloat16)
    plane_low = (in_plane - plane_high.astype(np.float32)).astype(jnp.bfloat16)
    f32, bf16 = jnp.float32, jnp.bfloat16
    vmem = pl.BlockSpec(memory_space=pltpu.VMEM)
    out = jax.ShapeDtypeStruct((1, bands, cells), f32)
    dma = pltpu.SemaphoreType.DMA
    field = pltpu.VMEM((bands, cells), f32)
    return pl.pallas_call(
        functools.partial(fused_kernel, atoms, slabs),
        out_shape=(out, out),
        in_specs=[vmem] * 8,
        out_specs=(vmem, vmem),
        scratch_shapes=[
            pltpu.VMEM((3, bands, cells), f32),
            pltpu.VMEM((rows, cells), bf16),
            pltpu.VMEM((rows, cells), bf16),
            pltpu.VMEM((bands, cells), bf16),
            pltpu.VMEM((bands, cells), bf16),
            pltpu.VMEM((3, 2, bands, cells), f32),
            field,
            field,
            field,
            pltpu.VMEM((3, bands, rows), f32),
            pltpu.VMEM((3, slabs, 8, rows), f32),
            pltpu.VMEM((3, 8, rows), f32),
            pltpu.VMEM((3, bands, rows), f32),
            pltpu.VMEM((8, every), f32),
            pltpu.VMEM((slabs, 8, every), f32),
            pltpu.VMEM((8, 128), f32),
            pltpu.VMEM((slabs, 8, 128), f32),
            dma((5,)),
            dma((5,)),
            dma((3, CHUNKS)),
            dma((3, CHUNKS)),
            dma((3, CHUNKS)),
            dma((3, CHUNKS)),
            dma((3, slabs)),
            dma((3, slabs)),
            dma((3, slabs)),
            dma((3, slabs)),
            dma((slabs,)),
            dma((slabs,)),
            dma((slabs,)),
            dma((slabs,)),
        ],
        compiler_params=pltpu.CompilerParams(
            collective_id=0, has_side_effects=True, vmem_limit_bytes=40 * 1024 * 1024
        ),
    )(
        occupied,
        start_guess[0],
        potential,
        perturbation,
        energy,
        fields,
        jnp.asarray(plane_high),
        jnp.asarray(plane_low),
    )


def local(
    occupied,
    start_guess,
    potential,
    perturbation,
    band_energy,
    beta_radial,
    beta_slope,
    atom_owner,
    atom_site,
    sphere_offset,
    displaced,
):
    slabs = lax.axis_size("dom")
    bands, cells = start_guess.shape[1:]
    atoms = atom_owner.shape[0]
    fields = atom_fields(
        slabs, cells, beta_radial, beta_slope, sphere_offset, atom_owner, atom_site, displaced
    )
    in_plane = plane_matrix()
    fits = bands == 8 * slabs and lax.axis_size("band") == 4 and atoms % 16 == 0 and atoms <= 112
    if fits and cells == HALO * PLANE:
        return fused(
            atoms,
            occupied,
            start_guess,
            potential[None, :],
            perturbation,
            band_energy[:, None],
            fields,
            in_plane,
        )
    answer, residual = plain(
        occupied,
        start_guess[0],
        potential[None, :],
        perturbation,
        band_energy[:, None],
        fields[:atoms],
        fields[atoms : atoms + 8],
        jnp.asarray(in_plane),
    )
    return answer[None], residual[None]


def solution(mesh):
    return jax.shard_map(
        local,
        mesh=mesh,
        in_specs=(
            P("band", "dom"),
            P(None, "band", "dom"),
            P("dom"),
            P(None, "dom"),
            P("band"),
            P(),
            P(),
            P(),
            P(),
            P(),
            P(),
        ),
        out_specs=(P(None, "band", "dom"), P(None, "band", "dom")),
        check_vma=False,
    )
```

```python
import functools
import numpy as np
import jax
import jax.numpy as jnp
from jax import lax
from jax.experimental import pallas as pl
from jax.experimental.pallas import tpu as pltpu
from jax.sharding import PartitionSpec as P

NY = 16
NX = 16
PLANE = NY * NX
HALO = 6
CHUNKS = 8
SUM_AT = 3
RAD = 5

COEF = (
    -5369.0 / 1800.0,
    12.0 / 7.0,
    -15.0 / 56.0,
    10.0 / 189.0,
    -1.0 / 112.0,
    2.0 / 825.0,
    -1.0 / 1386.0,
)
KINETIC = 2.0
SHIFT = 20.0
STRENGTH = 10.0
HIGH = lax.Precision.HIGHEST


def plane_matrix():
    full = np.zeros((PLANE, PLANE), np.float64)
    for y in range(NY):
        for x in range(NX):
            at = y * NX + x
            full[at, at] += 3.0 * COEF[0]
            for d in range(1, 7):
                for s in (d, -d):
                    full[((y + s) % NY) * NX + x, at] += COEF[d]
                    full[y * NX + (x + s) % NX, at] += COEF[d]
    return (-KINETIC * full).astype(np.float32)


def fields_kernel(slabs, depth, radial, slope, offset, owner, site, displaced, out, padded):
    atoms = owner.shape[0]
    planes = slabs * depth
    points = offset.shape[1]
    slab = lax.axis_index("dom")
    rows = lax.broadcasted_iota(jnp.int32, (16, points), 0)
    along_z = rows == offset[0:1, :] + RAD
    in_plane = (offset[1:2, :] & (NY - 1)) * NX + (offset[2:3, :] & (NX - 1))
    hot = jnp.where(
        lax.broadcasted_iota(jnp.int32, (PLANE, points), 0) == in_plane, 1.0, 0.0
    ).astype(jnp.float32)
    left = jnp.concatenate(
        [jnp.where(along_z, radial[...], 0.0), jnp.where(along_z, slope[...], 0.0)], axis=0
    )
    template = lax.dot_general(
        left, hot, (((1,), (1,)), ((), ())), precision=HIGH, preferred_element_type=jnp.float32
    )
    padded[...] = jnp.zeros_like(padded)
    for which in range(2):
        part = template[16 * which : 16 * which + 16]
        padded[which, 0:16, :] = part
        padded[which, planes : planes + 16, :] = part
    column = lax.broadcasted_iota(jnp.int32, (8, PLANE), 1) & (NX - 1)

    def shifted(which, a):
        z = lax.rem(slab * depth + RAD + 2 * planes - owner[a] * depth - site[0, a], planes)
        x = site[2, a]
        turn = site[1, a] * NX + x
        start = pl.multiple_of(lax.div(z, 8) * 8, 8)
        block = pltpu.roll(padded[which, pl.ds(start, 16), :], lax.rem(16 - lax.rem(z, 8), 16), 0)[0:8]
        first = pltpu.roll(block, turn, 1)
        second = pltpu.roll(block, lax.rem(turn + PLANE - NX, PLANE), 1)
        return jnp.where(column >= x, first, second)

    out[atoms:, :] = jnp.zeros((out.shape[0] - atoms, out.shape[1]), jnp.float32)
    for row in range(atoms + 2):
        field = shifted(0, row) if row < atoms else shifted(row - atoms, displaced[0])
        for z in range(depth):
            out[row : row + 1, z * PLANE : (z + 1) * PLANE] = field[z : z + 1]


def atom_fields(slabs, cells, beta_radial, beta_slope, offset, owner, site, displaced):
    atoms = owner.shape[0]
    depth = cells // PLANE
    vmem = pl.BlockSpec(memory_space=pltpu.VMEM)
    smem = pl.BlockSpec(memory_space=pltpu.SMEM)
    return pl.pallas_call(
        functools.partial(fields_kernel, slabs, depth),
        out_shape=jax.ShapeDtypeStruct((max(128, atoms + 16), cells), jnp.float32),
        in_specs=[vmem, vmem, vmem, smem, smem, smem],
        out_specs=vmem,
        scratch_shapes=[pltpu.VMEM((2, slabs * depth + 16, PLANE), jnp.float32)],
        compiler_params=pltpu.CompilerParams(vmem_limit_bytes=16 * 1024 * 1024),
    )(beta_radial[None, :], beta_slope[None, :], offset, owner, site, displaced)


def times(a, b, dims):
    return lax.dot_general(a, b, (dims, ((), ())), precision=HIGH, preferred_element_type=jnp.float32)


def plain(occupied, start, potential, perturbation, energy, beta, pair, in_plane):
    slabs = lax.axis_size("dom")
    bands, cells = start.shape
    depth = cells // PLANE
    total = cells * slabs
    whole = lax.all_gather(occupied, "band", axis=0, tiled=True)
    every = whole.shape[0]
    up = [(i, (i + 1) % slabs) for i in range(slabs)]
    down = [(j, i) for i, j in up]

    def local_part(field):
        before = lax.ppermute(field, "dom", up)
        after = lax.ppermute(field, "dom", down)
        grid = jnp.concatenate([before, field, after], axis=1)
        image = times(field.reshape(bands * depth, PLANE), in_plane, ((1,), (0,))).reshape(bands, cells)
        for d in range(1, 7):
            low = (depth - d) * PLANE
            high = (depth + d) * PLANE
            image += (-KINETIC * COEF[d]) * (grid[:, low : low + cells] + grid[:, high : high + cells])
        return image + (potential - energy) * field

    def correlate(field):
        return jnp.concatenate(
            [times(field, whole, ((1,), (1,))), times(field, beta, ((1,), (1,)))], axis=1
        )

    def operator(field, total_correlation):
        return (
            local_part(field)
            + (SHIFT / total) * times(total_correlation[:, :every], whole, ((1,), (0,)))
            + STRENGTH * times(total_correlation[:, every:], beta, ((1,), (0,)))
        )

    def dot(u, v):
        return jnp.sum(u * v, axis=1, keepdims=True)

    shaped = perturbation * occupied
    first, on_atoms, own, of_all = lax.psum(
        (
            times(shaped - SHIFT * start, whole, ((1,), (1,))),
            times(start, beta, ((1,), (1,))),
            times(occupied, pair, ((1,), (1,))),
            times(pair, whole, ((1,), (1,))),
        ),
        "dom",
    )
    own_radial, own_slope = own[:, 0:1], own[:, 1:2]
    first = first + STRENGTH * (own_radial * of_all[1:2] + own_slope * of_all[0:1])
    residual = (
        times(first * (1.0 / total), whole, ((1,), (0,)))
        - STRENGTH * times(on_atoms, beta, ((1,), (0,)))
        - local_part(start)
        - shaped
        - STRENGTH * (own_radial * pair[1:2] + own_slope * pair[0:1])
    )
    correlation, norm = lax.psum((correlate(residual), dot(residual, residual)), "dom")
    image = operator(residual, correlation)
    correlation, curve = lax.psum((correlate(image), dot(residual, image)), "dom")
    alpha = norm / curve
    again = operator(image, correlation)
    later = residual - alpha * image
    later_image = image - alpha * again
    new, bend, cross = lax.psum((dot(later, later), dot(later, later_image), dot(later, image)), "dom")
    ratio = new / norm
    step = new / (bend + ratio * (2.0 * cross + ratio * curve))
    answer = start + alpha * residual + step * (later + ratio * residual)
    return answer, later - step * (later_image + ratio * image)


NT = (((1,), (1,)), ((), ()))
NN = (((1,), (0,)), ((), ()))
MESH = pl.DeviceIdType.MESH


def parts_of(x):
    high = x.astype(jnp.bfloat16)
    return high, (x - high.astype(jnp.float32)).astype(jnp.bfloat16)


def product(a, b, dims):
    def one(u, v):
        return lax.dot_general(u, v, dims, preferred_element_type=jnp.float32)

    return one(a[0], b[0]) + (one(a[0], b[1]) + one(a[1], b[0]))


def fused_kernel(
    atoms,
    slabs,
    occ_in,
    start_in,
    pot,
    pert,
    energy,
    fields,
    answer,
    residual,
    occ,
    start,
    plane_high,
    plane_low,
    whole,
    w_high,
    w_low,
    f_high,
    f_low,
    faces,
    r0,
    w0,
    image,
    part,
    pieces,
    summed,
    totals,
    rows_part,
    rows_in,
    last_part,
    last_in,
    band_send,
    band_recv,
    face_send,
    face_recv,
    hand_send,
    hand_recv,
    sum_send,
    sum_recv,
    all_send,
    all_recv,
    rows_send,
    rows_recv,
    last_send,
    last_recv,
    local_sem,
):
    bands, cells = occ.shape
    every = 4 * bands
    total = cells * slabs
    band = lax.axis_index("band")
    slab = lax.axis_index("dom")
    sibling = band + 1 - 2 * (band % 2)
    across = (band + 2) % 4
    loads = [
        pltpu.make_async_copy(occ_in, occ, local_sem.at[0]),
        pltpu.make_async_copy(start_in, start, local_sem.at[1]),
    ]
    for load in loads:
        load.start()
    barrier = pltpu.get_barrier_semaphore()
    pl.semaphore_signal(barrier, inc=1, device_id={"band": sibling}, device_id_type=MESH)
    pl.semaphore_signal(barrier, inc=1, device_id={"band": across}, device_id_type=MESH)
    peers = [(slab + k) % slabs for k in range(slabs)]
    for k in range(1, slabs):
        pl.semaphore_signal(barrier, inc=1, device_id={"dom": peers[k]}, device_id_type=MESH)
    pl.semaphore_wait(barrier, slabs + 1)

    pending = []

    def send(src, dst, send_sem, recv_sem, device):
        copy = pltpu.make_async_remote_copy(
            src_ref=src,
            dst_ref=dst,
            send_sem=send_sem,
            recv_sem=recv_sem,
            device_id=device,
            device_id_type=MESH,
        )
        copy.start()
        pending.append(copy)
        return copy

    chunk = bands // CHUNKS
    side = slab % 2
    beside = slab + 1 - 2 * side
    beyond = (slab + slabs + 2 - 4 * side) % slabs

    def send_face(turn, field, c):
        return send(
            field.at[pl.ds(c * chunk, chunk)],
            faces.at[turn, side, pl.ds(c * chunk, chunk)],
            face_send.at[turn, c],
            face_recv.at[turn, c],
            {"dom": beside},
        )

    def hand_over(turn, c):
        return send(
            faces.at[turn, 1 - side, pl.ds(c * chunk, chunk)],
            faces.at[turn, side, pl.ds(c * chunk, chunk)],
            hand_send.at[turn, c],
            hand_recv.at[turn, c],
            {"dom": beyond},
        )

    def hand_on(turn, copies, c):
        copies[c].wait_recv()
        copies.append(hand_over(turn, c))

    half = bands // 2
    crossing = [
        send(
            occ_in.at[pl.ds(c * half, half)],
            whole.at[1, pl.ds(c * half, half)],
            band_send.at[c],
            band_recv.at[c],
            {"band": across},
        )
        for c in range(2)
    ]
    to_sibling = send(occ_in, whole.at[0], band_send.at[2], band_recv.at[2], {"band": sibling})
    moving = [send_face(0, start_in, c) for c in range(CHUNKS)]

    def hold(row, block):
        high, low = parts_of(block)
        w_high[row : row + block.shape[0], :] = high
        w_low[row : row + block.shape[0], :] = low

    def hold_field(block):
        high, low = parts_of(block)
        f_high[...] = high
        f_low[...] = low

    def plane_image(field, planes):
        for z in planes:
            cut = slice(z * PLANE, (z + 1) * PLANE)
            image[:, cut] = product(
                (f_high[:, cut], f_low[:, cut]), (plane_high[...], plane_low[...]), NN
            ) + (pot[:, cut] - energy[...]) * field[:, cut]

    def across_planes(turn, field, c):
        def group(i, carry):
            rows = pl.ds(pl.multiple_of(i * 8, 8), 8)
            grid = [
                ref[rows, z * PLANE : (z + 1) * PLANE]
                for ref in (faces.at[turn, 0], field, faces.at[turn, 1])
                for z in range(HALO)
            ]
            for z in range(HALO):
                cut = slice(z * PLANE, (z + 1) * PLANE)
                value = image[rows, cut]
                for d in range(1, 7):
                    value += (-KINETIC * COEF[d]) * (grid[HALO + z - d] + grid[HALO + z + d])
                image[rows, cut] = value
            return carry

        lax.fori_loop(c * chunk // 8, (c + 1) * chunk // 8, group, 0)

    def start_sum(turn):
        return [
            send(
                part.at[turn, pl.ds(pl.multiple_of(peers[k] * 8, 8), 8)],
                pieces.at[turn, k],
                sum_send.at[turn, k],
                sum_recv.at[turn, k],
                {"dom": peers[k]},
            )
            for k in range(1, slabs)
        ]

    def share_sum(turn, copies):
        mine = pl.ds(pl.multiple_of(slab * 8, 8), 8)
        value = part[turn, mine, :]
        for k in range(1, slabs):
            copies[k - 1].wait_recv()
            value += pieces[turn, k]
        summed[turn] = value
        shared = [
            send(
                summed.at[turn],
                totals.at[turn, mine],
                all_send.at[turn, k],
                all_recv.at[turn, k],
                {"dom": peers[k]},
            )
            for k in range(1, slabs)
        ]
        totals[turn, mine, :] = value
        return shared

    def finish_sum(shared):
        for copy in shared:
            copy.wait_recv()

    lane = lax.broadcasted_iota(jnp.int32, (bands, 128), 1)

    def correlate(rows):
        return product((f_high[...], f_low[...]), (w_high[rows, :], w_low[rows, :]), NT)

    def back(coefficients):
        return product(parts_of(coefficients), (w_high[...], w_low[...]), NN)

    one_cell = lax.broadcasted_iota(jnp.int32, (PLANE, PLANE), 0)
    other_cell = lax.broadcasted_iota(jnp.int32, (PLANE, PLANE), 1)
    along_x = (one_cell - other_cell) & (NX - 1)
    along_y = ((one_cell >> 4) - (other_cell >> 4)) & (NY - 1)
    away_x = jnp.minimum(along_x, NX - along_x)
    away_y = jnp.minimum(along_y, NY - along_y)
    away = jnp.where(away_x == 0, away_y, jnp.where(away_y == 0, away_x, NX))
    matrix = jnp.where(away == 0, -KINETIC * 3.0 * COEF[0], 0.0)
    for d in range(1, 7):
        matrix = jnp.where(away == d, -KINETIC * COEF[d], matrix)
    matrix_high, matrix_low = parts_of(matrix.astype(jnp.float32))
    plane_high[...] = matrix_high
    plane_low[...] = matrix_low

    for load in loads:
        load.wait()
    hold(0, occ[...])
    hold(every, fields[...])
    hold_field(start[...])
    plane_image(start, range(HALO))
    hand_on(0, moving, 0)
    hand_on(0, moving, 1)
    ends = slice(every, every + 128)
    on_start = correlate(ends)
    on_own = product(
        (w_high[0:bands, :], w_low[0:bands, :]), (w_high[ends, :], w_low[ends, :]), NT
    )
    part[0, :, every:] = jnp.where(lane < atoms, on_start, on_own)
    hand_on(0, moving, 2)
    shaped = pert[...] * occ[...]
    hold_field(shaped - SHIFT * start[...])
    to_sibling.wait_recv()
    hold(bands, whole[0])
    hand_on(0, moving, 3)
    part[0, :, 0 : 2 * bands] = correlate(slice(0, 2 * bands))
    passed = []
    for c in range(2):
        crossing[c].wait_recv()
        passed.append(
            send(
                whole.at[1, pl.ds(c * half, half)],
                whole.at[2, pl.ds(c * half, half)],
                band_send.at[3 + c],
                band_recv.at[3 + c],
                {"band": sibling},
            )
        )
        hand_on(0, moving, 4 + 2 * c)
        hand_on(0, moving, 5 + 2 * c)
    hold(2 * bands, whole[1])
    for copy in passed:
        copy.wait_recv()
    hold(3 * bands, whole[2])
    part[0, :, 2 * bands : every] = correlate(slice(2 * bands, every))
    copies = start_sum(0)
    pair = slice(every + atoms, every + atoms + 16)
    rows_part[...] = product(
        (w_high[pair, :], w_low[pair, :]), (w_high[0:every, :], w_low[0:every, :]), NT
    )[0:8]
    row_copies = [
        send(rows_part, rows_in.at[k], rows_send.at[k], rows_recv.at[k], {"dom": peers[k]})
        for k in range(1, slabs)
    ]
    shared = share_sum(0, copies)
    for c in range(CHUNKS):
        moving[CHUNKS + c].wait_recv()
        across_planes(0, start, c)
    of_all = rows_part[...]
    for k in range(1, slabs):
        row_copies[k - 1].wait_recv()
        of_all += rows_in[k]
    finish_sum(shared)
    last = totals[0, :, every:]
    own_radial, own_slope = last[:, atoms : atoms + 1], last[:, atoms + 1 : atoms + 2]
    first = totals[0, :, 0:every] + STRENGTH * (own_radial * of_all[1:2] + own_slope * of_all[0:1])
    ends_part = jnp.where(
        lane < atoms,
        last,
        jnp.where(lane == atoms, own_slope, jnp.where(lane == atoms + 1, own_radial, 0.0)),
    )
    r0[...] = (
        back(jnp.concatenate([first * (1.0 / total), -STRENGTH * ends_part], axis=1))
        - image[...]
        - pert[...] * occ[...]
    )

    def apply(turn, field, scalar):
        moving = [send_face(turn, field, c) for c in range(2)]
        hold_field(field[...])
        part[turn, :, 0:every] = correlate(slice(0, every))
        part[turn, :, every:] = jnp.where(lane == atoms, scalar, correlate(ends))
        copies = start_sum(turn)
        face = list(moving)
        handed = []
        for c in range(CHUNKS):
            if c + 2 < CHUNKS:
                face.append(send_face(turn, field, c + 2))
            face[c].wait_recv()
            handed.append(hand_over(turn, c))
            if c < 3:
                plane_image(field, range(2 * c, 2 * c + 2))
            if c == SUM_AT:
                shared = share_sum(turn, copies)
            if c >= 4:
                handed[c - 4].wait_recv()
                across_planes(turn, field, c - 4)
        for c in range(CHUNKS - 4, CHUNKS):
            handed[c].wait_recv()
            across_planes(turn, field, c)
        finish_sum(shared)
        last = totals[turn, :, every:]
        coefficients = jnp.concatenate(
            [
                totals[turn, :, 0:every] * (SHIFT / total),
                jnp.where(lane < atoms, STRENGTH * last, 0.0),
            ],
            axis=1,
        )
        image[...] += back(coefficients)
        return last[:, atoms : atoms + 1]

    def dot(u, v):
        return jnp.sum(u * v, axis=1, keepdims=True)

    norm = apply(1, r0, dot(r0[...], r0[...]))
    w0[...] = image[...]
    curve = apply(2, w0, dot(r0[...], w0[...]))
    alpha = norm / curve
    later = r0[...] - alpha * w0[...]
    later_image = w0[...] - alpha * image[...]
    residual[0] = later
    image[...] = later_image
    three = jnp.where(
        lane == 0,
        dot(later, later),
        jnp.where(
            lane == 1, dot(later, later_image), jnp.where(lane == 2, dot(later, w0[...]), 0.0)
        ),
    )
    eye = jnp.where(
        lax.broadcasted_iota(jnp.int32, (128, 128), 0)
        == lax.broadcasted_iota(jnp.int32, (128, 128), 1),
        1.0,
        0.0,
    ).astype(jnp.float32)
    three = jnp.concatenate([three, jnp.zeros((128 - bands, 128), jnp.float32)], axis=0)
    last_part[...] = lax.dot_general(
        eye[0:8], three, NT, precision=HIGH, preferred_element_type=jnp.float32
    )
    last_copies = [
        send(last_part, last_in.at[k], last_send.at[k], last_recv.at[k], {"dom": peers[k]})
        for k in range(1, slabs)
    ]
    value = last_part[...]
    for k in range(1, slabs):
        last_copies[k - 1].wait_recv()
        value += last_in[k]
    three = lax.dot_general(
        eye[0:bands], value, NT, precision=HIGH, preferred_element_type=jnp.float32
    )
    new, bend, cross = three[:, 0:1], three[:, 1:2], three[:, 2:3]
    ratio = new / norm
    step = new / (bend + ratio * (2.0 * cross + ratio * curve))
    later = residual[0]
    answer[0] = start[...] + alpha * r0[...] + step * (later + ratio * r0[...])
    residual[0] = later - step * (image[...] + ratio * w0[...])
    for copy in pending:
        copy.wait_send()


def fused(atoms, occupied, start_guess, potential, perturbation, energy, fields):
    slabs = lax.axis_size("dom")
    bands, cells = occupied.shape
    every = 4 * bands
    rows = every + 128
    f32, bf16 = jnp.float32, jnp.bfloat16
    vmem = pl.BlockSpec(memory_space=pltpu.VMEM)
    out = jax.ShapeDtypeStruct((1, bands, cells), f32)
    dma = pltpu.SemaphoreType.DMA
    field = pltpu.VMEM((bands, cells), f32)
    return pl.pallas_call(
        functools.partial(fused_kernel, atoms, slabs),
        out_shape=(out, out),
        in_specs=[pl.BlockSpec(memory_space=pl.ANY)] * 2 + [vmem] * 4,
        out_specs=(vmem, vmem),
        scratch_shapes=[
            field,
            field,
            pltpu.VMEM((PLANE, PLANE), bf16),
            pltpu.VMEM((PLANE, PLANE), bf16),
            pltpu.VMEM((3, bands, cells), f32),
            pltpu.VMEM((rows, cells), bf16),
            pltpu.VMEM((rows, cells), bf16),
            pltpu.VMEM((bands, cells), bf16),
            pltpu.VMEM((bands, cells), bf16),
            pltpu.VMEM((3, 2, bands, cells), f32),
            field,
            field,
            field,
            pltpu.VMEM((3, bands, rows), f32),
            pltpu.VMEM((3, slabs, 8, rows), f32),
            pltpu.VMEM((3, 8, rows), f32),
            pltpu.VMEM((3, bands, rows), f32),
            pltpu.VMEM((8, every), f32),
            pltpu.VMEM((slabs, 8, every), f32),
            pltpu.VMEM((8, 128), f32),
            pltpu.VMEM((slabs, 8, 128), f32),
            dma((5,)),
            dma((5,)),
            dma((3, CHUNKS)),
            dma((3, CHUNKS)),
            dma((3, CHUNKS)),
            dma((3, CHUNKS)),
            dma((3, slabs)),
            dma((3, slabs)),
            dma((3, slabs)),
            dma((3, slabs)),
            dma((slabs,)),
            dma((slabs,)),
            dma((slabs,)),
            dma((slabs,)),
            dma((2,)),
        ],
        compiler_params=pltpu.CompilerParams(
            collective_id=0, has_side_effects=True, vmem_limit_bytes=40 * 1024 * 1024
        ),
    )(
        occupied,
        start_guess[0],
        potential,
        perturbation,
        energy,
        fields,
    )


def local(
    occupied,
    start_guess,
    potential,
    perturbation,
    band_energy,
    beta_radial,
    beta_slope,
    atom_owner,
    atom_site,
    sphere_offset,
    displaced,
):
    slabs = lax.axis_size("dom")
    bands, cells = start_guess.shape[1:]
    atoms = atom_owner.shape[0]
    fields = atom_fields(
        slabs, cells, beta_radial, beta_slope, sphere_offset, atom_owner, atom_site, displaced
    )
    fits = bands == 8 * slabs and lax.axis_size("band") == 4 and atoms % 16 == 0 and atoms <= 112
    if fits and cells == HALO * PLANE:
        return fused(
            atoms,
            occupied,
            start_guess,
            potential[None, :],
            perturbation,
            band_energy[:, None],
            fields,
        )
    answer, residual = plain(
        occupied,
        start_guess[0],
        potential[None, :],
        perturbation,
        band_energy[:, None],
        fields[:atoms],
        fields[atoms : atoms + 8],
        jnp.asarray(plane_matrix()),
    )
    return answer[None], residual[None]


def solution(mesh):
    return jax.shard_map(
        local,
        mesh=mesh,
        in_specs=(
            P("band", "dom"),
            P(None, "band", "dom"),
            P("dom"),
            P(None, "dom"),
            P("band"),
            P(),
            P(),
            P(),
            P(),
            P(),
            P(),
        ),
        out_specs=(P(None, "band", "dom"), P(None, "band", "dom")),
        check_vma=False,
    )
```

```python
import functools
import numpy as np
import jax
import jax.numpy as jnp
from jax import lax
from jax.experimental import pallas as pl
from jax.experimental.pallas import tpu as pltpu
from jax.sharding import PartitionSpec as P

NY = 16
NX = 16
PLANE = NY * NX
HALO = 6
CHUNKS = 8
SUM_AT = 3
RAD = 5

COEF = (
    -5369.0 / 1800.0,
    12.0 / 7.0,
    -15.0 / 56.0,
    10.0 / 189.0,
    -1.0 / 112.0,
    2.0 / 825.0,
    -1.0 / 1386.0,
)
KINETIC = 2.0
SHIFT = 20.0
STRENGTH = 10.0
HIGH = lax.Precision.HIGHEST


def plane_matrix():
    full = np.zeros((PLANE, PLANE), np.float64)
    for y in range(NY):
        for x in range(NX):
            at = y * NX + x
            full[at, at] += 3.0 * COEF[0]
            for d in range(1, 7):
                for s in (d, -d):
                    full[((y + s) % NY) * NX + x, at] += COEF[d]
                    full[y * NX + (x + s) % NX, at] += COEF[d]
    return (-KINETIC * full).astype(np.float32)


def fields_kernel(slabs, depth, radial, slope, offset, owner, site, displaced, out, padded):
    atoms = owner.shape[0]
    planes = slabs * depth
    points = offset.shape[1]
    slab = lax.axis_index("dom")
    rows = lax.broadcasted_iota(jnp.int32, (16, points), 0)
    along_z = rows == offset[0:1, :] + RAD
    in_plane = (offset[1:2, :] & (NY - 1)) * NX + (offset[2:3, :] & (NX - 1))
    hot = jnp.where(
        lax.broadcasted_iota(jnp.int32, (PLANE, points), 0) == in_plane, 1.0, 0.0
    ).astype(jnp.float32)
    left = jnp.concatenate(
        [jnp.where(along_z, radial[...], 0.0), jnp.where(along_z, slope[...], 0.0)], axis=0
    )
    template = lax.dot_general(
        left, hot, (((1,), (1,)), ((), ())), precision=HIGH, preferred_element_type=jnp.float32
    )
    padded[...] = jnp.zeros_like(padded)
    for which in range(2):
        part = template[16 * which : 16 * which + 16]
        padded[which, 0:16, :] = part
        padded[which, planes : planes + 16, :] = part
    column = lax.broadcasted_iota(jnp.int32, (8, PLANE), 1) & (NX - 1)

    def shifted(which, a):
        z = lax.rem(slab * depth + RAD + 2 * planes - owner[a] * depth - site[0, a], planes)
        x = site[2, a]
        turn = site[1, a] * NX + x
        start = pl.multiple_of(lax.div(z, 8) * 8, 8)
        block = pltpu.roll(padded[which, pl.ds(start, 16), :], lax.rem(16 - lax.rem(z, 8), 16), 0)[0:8]
        first = pltpu.roll(block, turn, 1)
        second = pltpu.roll(block, lax.rem(turn + PLANE - NX, PLANE), 1)
        return jnp.where(column >= x, first, second)

    out[atoms:, :] = jnp.zeros((out.shape[0] - atoms, out.shape[1]), jnp.float32)
    for row in range(atoms + 2):
        field = shifted(0, row) if row < atoms else shifted(row - atoms, displaced[0])
        for z in range(depth):
            out[row : row + 1, z * PLANE : (z + 1) * PLANE] = field[z : z + 1]


def atom_fields(slabs, cells, beta_radial, beta_slope, offset, owner, site, displaced):
    atoms = owner.shape[0]
    depth = cells // PLANE
    vmem = pl.BlockSpec(memory_space=pltpu.VMEM)
    smem = pl.BlockSpec(memory_space=pltpu.SMEM)
    return pl.pallas_call(
        functools.partial(fields_kernel, slabs, depth),
        out_shape=jax.ShapeDtypeStruct((max(128, atoms + 16), cells), jnp.float32),
        in_specs=[vmem, vmem, vmem, smem, smem, smem],
        out_specs=vmem,
        scratch_shapes=[pltpu.VMEM((2, slabs * depth + 16, PLANE), jnp.float32)],
        compiler_params=pltpu.CompilerParams(vmem_limit_bytes=16 * 1024 * 1024),
    )(beta_radial[None, :], beta_slope[None, :], offset, owner, site, displaced)


def times(a, b, dims):
    return lax.dot_general(a, b, (dims, ((), ())), precision=HIGH, preferred_element_type=jnp.float32)


def plain(occupied, start, potential, perturbation, energy, beta, pair, in_plane):
    slabs = lax.axis_size("dom")
    bands, cells = start.shape
    depth = cells // PLANE
    total = cells * slabs
    whole = lax.all_gather(occupied, "band", axis=0, tiled=True)
    every = whole.shape[0]
    up = [(i, (i + 1) % slabs) for i in range(slabs)]
    down = [(j, i) for i, j in up]

    def local_part(field):
        before = lax.ppermute(field, "dom", up)
        after = lax.ppermute(field, "dom", down)
        grid = jnp.concatenate([before, field, after], axis=1)
        image = times(field.reshape(bands * depth, PLANE), in_plane, ((1,), (0,))).reshape(bands, cells)
        for d in range(1, 7):
            low = (depth - d) * PLANE
            high = (depth + d) * PLANE
            image += (-KINETIC * COEF[d]) * (grid[:, low : low + cells] + grid[:, high : high + cells])
        return image + (potential - energy) * field

    def correlate(field):
        return jnp.concatenate(
            [times(field, whole, ((1,), (1,))), times(field, beta, ((1,), (1,)))], axis=1
        )

    def operator(field, total_correlation):
        return (
            local_part(field)
            + (SHIFT / total) * times(total_correlation[:, :every], whole, ((1,), (0,)))
            + STRENGTH * times(total_correlation[:, every:], beta, ((1,), (0,)))
        )

    def dot(u, v):
        return jnp.sum(u * v, axis=1, keepdims=True)

    shaped = perturbation * occupied
    first, on_atoms, own, of_all = lax.psum(
        (
            times(shaped - SHIFT * start, whole, ((1,), (1,))),
            times(start, beta, ((1,), (1,))),
            times(occupied, pair, ((1,), (1,))),
            times(pair, whole, ((1,), (1,))),
        ),
        "dom",
    )
    own_radial, own_slope = own[:, 0:1], own[:, 1:2]
    first = first + STRENGTH * (own_radial * of_all[1:2] + own_slope * of_all[0:1])
    residual = (
        times(first * (1.0 / total), whole, ((1,), (0,)))
        - STRENGTH * times(on_atoms, beta, ((1,), (0,)))
        - local_part(start)
        - shaped
        - STRENGTH * (own_radial * pair[1:2] + own_slope * pair[0:1])
    )
    correlation, norm = lax.psum((correlate(residual), dot(residual, residual)), "dom")
    image = operator(residual, correlation)
    correlation, curve = lax.psum((correlate(image), dot(residual, image)), "dom")
    alpha = norm / curve
    again = operator(image, correlation)
    later = residual - alpha * image
    later_image = image - alpha * again
    new, bend, cross = lax.psum((dot(later, later), dot(later, later_image), dot(later, image)), "dom")
    ratio = new / norm
    step = new / (bend + ratio * (2.0 * cross + ratio * curve))
    answer = start + alpha * residual + step * (later + ratio * residual)
    return answer, later - step * (later_image + ratio * image)


NT = (((1,), (1,)), ((), ()))
NN = (((1,), (0,)), ((), ()))
MESH = pl.DeviceIdType.MESH


def parts_of(x):
    high = x.astype(jnp.bfloat16)
    return high, (x - high.astype(jnp.float32)).astype(jnp.bfloat16)


def product(a, b, dims):
    def one(u, v):
        return lax.dot_general(u, v, dims, preferred_element_type=jnp.float32)

    return one(a[0], b[0]) + (one(a[0], b[1]) + one(a[1], b[0]))


def fused_kernel(
    atoms,
    slabs,
    occ_in,
    start_in,
    pot,
    pert,
    energy,
    fields,
    answer,
    residual,
    occ,
    start,
    plane_high,
    plane_low,
    whole,
    w_high,
    w_low,
    f_high,
    f_low,
    faces,
    r0,
    w0,
    image,
    part,
    pieces,
    summed,
    totals,
    rows_part,
    rows_in,
    last_part,
    last_in,
    band_send,
    band_recv,
    face_send,
    face_recv,
    hand_send,
    hand_recv,
    sum_send,
    sum_recv,
    all_send,
    all_recv,
    rows_send,
    rows_recv,
    last_send,
    last_recv,
    local_sem,
):
    bands, cells = occ.shape
    every = 4 * bands
    total = cells * slabs
    band = lax.axis_index("band")
    slab = lax.axis_index("dom")
    sibling = band + 1 - 2 * (band % 2)
    across = (band + 2) % 4
    loads = [
        pltpu.make_async_copy(occ_in, occ, local_sem.at[0]),
        pltpu.make_async_copy(start_in, start, local_sem.at[1]),
    ]
    for load in loads:
        load.start()
    barrier = pltpu.get_barrier_semaphore()
    pl.semaphore_signal(barrier, inc=1, device_id={"band": sibling}, device_id_type=MESH)
    pl.semaphore_signal(barrier, inc=1, device_id={"band": across}, device_id_type=MESH)
    peers = [(slab + k) % slabs for k in range(slabs)]
    for k in range(1, slabs):
        pl.semaphore_signal(barrier, inc=1, device_id={"dom": peers[k]}, device_id_type=MESH)
    pl.semaphore_wait(barrier, slabs + 1)

    pending = []

    def send(src, dst, send_sem, recv_sem, device):
        copy = pltpu.make_async_remote_copy(
            src_ref=src,
            dst_ref=dst,
            send_sem=send_sem,
            recv_sem=recv_sem,
            device_id=device,
            device_id_type=MESH,
        )
        copy.start()
        pending.append(copy)
        return copy

    chunk = bands // CHUNKS
    side = slab % 2
    beside = slab + 1 - 2 * side
    beyond = (slab + slabs + 2 - 4 * side) % slabs

    def send_face(turn, field, c):
        return send(
            field.at[pl.ds(c * chunk, chunk)],
            faces.at[turn, side, pl.ds(c * chunk, chunk)],
            face_send.at[turn, c],
            face_recv.at[turn, c],
            {"dom": beside},
        )

    def hand_over(turn, c):
        return send(
            faces.at[turn, 1 - side, pl.ds(c * chunk, chunk)],
            faces.at[turn, side, pl.ds(c * chunk, chunk)],
            hand_send.at[turn, c],
            hand_recv.at[turn, c],
            {"dom": beyond},
        )

    def hand_on(turn, copies, c):
        copies[c].wait_recv()
        copies.append(hand_over(turn, c))

    half = bands // 2
    crossing = [
        send(
            occ_in.at[pl.ds(c * half, half)],
            whole.at[1, pl.ds(c * half, half)],
            band_send.at[c],
            band_recv.at[c],
            {"band": across},
        )
        for c in range(2)
    ]
    to_sibling = send(occ_in, whole.at[0], band_send.at[2], band_recv.at[2], {"band": sibling})
    moving = [send_face(0, start_in, c) for c in range(CHUNKS)]

    def hold(row, block):
        high, low = parts_of(block)
        w_high[row : row + block.shape[0], :] = high
        w_low[row : row + block.shape[0], :] = low

    def hold_field(block):
        high, low = parts_of(block)
        f_high[...] = high
        f_low[...] = low

    def plane_image(field, planes):
        for z in planes:
            cut = slice(z * PLANE, (z + 1) * PLANE)
            image[:, cut] = product(
                (f_high[:, cut], f_low[:, cut]), (plane_high[...], plane_low[...]), NN
            ) + (pot[:, cut] - energy[...]) * field[:, cut]

    def across_planes(turn, field, c):
        def group(i, carry):
            rows = pl.ds(pl.multiple_of(i * 8, 8), 8)
            grid = [
                ref[rows, z * PLANE : (z + 1) * PLANE]
                for ref in (faces.at[turn, 0], field, faces.at[turn, 1])
                for z in range(HALO)
            ]
            for z in range(HALO):
                cut = slice(z * PLANE, (z + 1) * PLANE)
                value = image[rows, cut]
                for d in range(1, 7):
                    value += (-KINETIC * COEF[d]) * (grid[HALO + z - d] + grid[HALO + z + d])
                image[rows, cut] = value
            return carry

        lax.fori_loop(c * chunk // 8, (c + 1) * chunk // 8, group, 0)

    def start_sum(turn):
        return [
            send(
                part.at[turn, pl.ds(pl.multiple_of(peers[k] * 8, 8), 8)],
                pieces.at[turn, k],
                sum_send.at[turn, k],
                sum_recv.at[turn, k],
                {"dom": peers[k]},
            )
            for k in range(1, slabs)
        ]

    def share_sum(turn, copies):
        mine = pl.ds(pl.multiple_of(slab * 8, 8), 8)
        value = part[turn, mine, :]
        for k in range(1, slabs):
            copies[k - 1].wait_recv()
            value += pieces[turn, k]
        summed[turn] = value
        shared = [
            send(
                summed.at[turn],
                totals.at[turn, mine],
                all_send.at[turn, k],
                all_recv.at[turn, k],
                {"dom": peers[k]},
            )
            for k in range(1, slabs)
        ]
        totals[turn, mine, :] = value
        return shared

    def finish_sum(shared):
        for copy in shared:
            copy.wait_recv()

    lane = lax.broadcasted_iota(jnp.int32, (bands, 128), 1)

    def correlate(rows):
        return product((f_high[...], f_low[...]), (w_high[rows, :], w_low[rows, :]), NT)

    def back(coefficients):
        return product(parts_of(coefficients), (w_high[...], w_low[...]), NN)

    one_cell = lax.broadcasted_iota(jnp.int32, (PLANE, PLANE), 0)
    other_cell = lax.broadcasted_iota(jnp.int32, (PLANE, PLANE), 1)
    along_x = (one_cell - other_cell) & (NX - 1)
    along_y = ((one_cell >> 4) - (other_cell >> 4)) & (NY - 1)
    away_x = jnp.minimum(along_x, NX - along_x)
    away_y = jnp.minimum(along_y, NY - along_y)
    away = jnp.where(away_x == 0, away_y, jnp.where(away_y == 0, away_x, NX))
    matrix = jnp.where(away == 0, -KINETIC * 3.0 * COEF[0], 0.0)
    for d in range(1, 7):
        matrix = jnp.where(away == d, -KINETIC * COEF[d], matrix)
    matrix_high, matrix_low = parts_of(matrix.astype(jnp.float32))
    plane_high[...] = matrix_high
    plane_low[...] = matrix_low

    for load in loads:
        load.wait()
    hold(0, occ[...])
    hold(every, fields[...])
    hold_field(start[...])
    plane_image(start, range(HALO))
    hand_on(0, moving, 0)
    hand_on(0, moving, 1)
    ends = slice(every, every + 128)
    on_start = correlate(ends)
    on_own = product(
        (w_high[0:bands, :], w_low[0:bands, :]), (w_high[ends, :], w_low[ends, :]), NT
    )
    part[0, :, every:] = jnp.where(lane < atoms, on_start, on_own)
    hand_on(0, moving, 2)
    shaped = pert[...] * occ[...]
    hold_field(shaped - SHIFT * start[...])
    to_sibling.wait_recv()
    hold(bands, whole[0])
    hand_on(0, moving, 3)
    part[0, :, 0 : 2 * bands] = correlate(slice(0, 2 * bands))
    passed = []
    for c in range(2):
        crossing[c].wait_recv()
        passed.append(
            send(
                whole.at[1, pl.ds(c * half, half)],
                whole.at[2, pl.ds(c * half, half)],
                band_send.at[3 + c],
                band_recv.at[3 + c],
                {"band": sibling},
            )
        )
        hand_on(0, moving, 4 + 2 * c)
        hand_on(0, moving, 5 + 2 * c)
    hold(2 * bands, whole[1])
    for copy in passed:
        copy.wait_recv()
    hold(3 * bands, whole[2])
    part[0, :, 2 * bands : every] = correlate(slice(2 * bands, every))
    copies = start_sum(0)
    pair = slice(every + atoms, every + atoms + 16)
    rows_part[...] = product(
        (w_high[pair, :], w_low[pair, :]), (w_high[0:every, :], w_low[0:every, :]), NT
    )[0:8]
    row_copies = [
        send(rows_part, rows_in.at[k], rows_send.at[k], rows_recv.at[k], {"dom": peers[k]})
        for k in range(1, slabs)
    ]
    shared = share_sum(0, copies)
    for c in range(CHUNKS):
        moving[CHUNKS + c].wait_recv()
        across_planes(0, start, c)
    of_all = rows_part[...]
    for k in range(1, slabs):
        row_copies[k - 1].wait_recv()
        of_all += rows_in[k]
    finish_sum(shared)
    last = totals[0, :, every:]
    own_radial, own_slope = last[:, atoms : atoms + 1], last[:, atoms + 1 : atoms + 2]
    first = totals[0, :, 0:every] + STRENGTH * (own_radial * of_all[1:2] + own_slope * of_all[0:1])
    ends_part = jnp.where(
        lane < atoms,
        last,
        jnp.where(lane == atoms, own_slope, jnp.where(lane == atoms + 1, own_radial, 0.0)),
    )
    r0[...] = (
        back(jnp.concatenate([first * (1.0 / total), -STRENGTH * ends_part], axis=1))
        - image[...]
        - pert[...] * occ[...]
    )

    def apply(turn, field, scalar):
        moving = [send_face(turn, field, c) for c in range(2)]
        hold_field(field[...])
        part[turn, :, 0:every] = correlate(slice(0, every))
        part[turn, :, every:] = jnp.where(lane == atoms, scalar, correlate(ends))
        copies = start_sum(turn)
        face = list(moving)
        handed = []
        for c in range(CHUNKS):
            if c + 2 < CHUNKS:
                face.append(send_face(turn, field, c + 2))
            face[c].wait_recv()
            handed.append(hand_over(turn, c))
            if c < 3:
                plane_image(field, range(2 * c, 2 * c + 2))
            if c == SUM_AT:
                shared = share_sum(turn, copies)
            if c >= 4:
                handed[c - 4].wait_recv()
                across_planes(turn, field, c - 4)
        finish_sum(shared)
        last = totals[turn, :, every:]
        coefficients = jnp.concatenate(
            [
                totals[turn, :, 0:every] * (SHIFT / total),
                jnp.where(lane < atoms, STRENGTH * last, 0.0),
            ],
            axis=1,
        )
        image[...] += back(coefficients)
        for c in range(CHUNKS - 4, CHUNKS):
            handed[c].wait_recv()
            across_planes(turn, field, c)
        return last[:, atoms : atoms + 1]

    def dot(u, v):
        return jnp.sum(u * v, axis=1, keepdims=True)

    norm = apply(1, r0, dot(r0[...], r0[...]))
    w0[...] = image[...]
    curve = apply(2, w0, dot(r0[...], w0[...]))
    alpha = norm / curve
    later = r0[...] - alpha * w0[...]
    later_image = w0[...] - alpha * image[...]
    residual[0] = later
    image[...] = later_image
    three = jnp.where(
        lane == 0,
        dot(later, later),
        jnp.where(
            lane == 1, dot(later, later_image), jnp.where(lane == 2, dot(later, w0[...]), 0.0)
        ),
    )
    eye = jnp.where(
        lax.broadcasted_iota(jnp.int32, (128, 128), 0)
        == lax.broadcasted_iota(jnp.int32, (128, 128), 1),
        1.0,
        0.0,
    ).astype(jnp.float32)
    three = jnp.concatenate([three, jnp.zeros((128 - bands, 128), jnp.float32)], axis=0)
    last_part[...] = lax.dot_general(
        eye[0:8], three, NT, precision=HIGH, preferred_element_type=jnp.float32
    )
    last_copies = [
        send(last_part, last_in.at[k], last_send.at[k], last_recv.at[k], {"dom": peers[k]})
        for k in range(1, slabs)
    ]
    value = last_part[...]
    for k in range(1, slabs):
        last_copies[k - 1].wait_recv()
        value += last_in[k]
    three = lax.dot_general(
        eye[0:bands], value, NT, precision=HIGH, preferred_element_type=jnp.float32
    )
    new, bend, cross = three[:, 0:1], three[:, 1:2], three[:, 2:3]
    ratio = new / norm
    step = new / (bend + ratio * (2.0 * cross + ratio * curve))
    later = residual[0]
    answer[0] = start[...] + alpha * r0[...] + step * (later + ratio * r0[...])
    residual[0] = later - step * (image[...] + ratio * w0[...])
    for copy in pending:
        copy.wait_send()


def fused(atoms, occupied, start_guess, potential, perturbation, energy, fields):
    slabs = lax.axis_size("dom")
    bands, cells = occupied.shape
    every = 4 * bands
    rows = every + 128
    f32, bf16 = jnp.float32, jnp.bfloat16
    vmem = pl.BlockSpec(memory_space=pltpu.VMEM)
    out = jax.ShapeDtypeStruct((1, bands, cells), f32)
    dma = pltpu.SemaphoreType.DMA
    field = pltpu.VMEM((bands, cells), f32)
    return pl.pallas_call(
        functools.partial(fused_kernel, atoms, slabs),
        out_shape=(out, out),
        in_specs=[pl.BlockSpec(memory_space=pl.ANY)] * 2 + [vmem] * 4,
        out_specs=(vmem, vmem),
        scratch_shapes=[
            field,
            field,
            pltpu.VMEM((PLANE, PLANE), bf16),
            pltpu.VMEM((PLANE, PLANE), bf16),
            pltpu.VMEM((3, bands, cells), f32),
            pltpu.VMEM((rows, cells), bf16),
            pltpu.VMEM((rows, cells), bf16),
            pltpu.VMEM((bands, cells), bf16),
            pltpu.VMEM((bands, cells), bf16),
            pltpu.VMEM((3, 2, bands, cells), f32),
            field,
            field,
            field,
            pltpu.VMEM((3, bands, rows), f32),
            pltpu.VMEM((3, slabs, 8, rows), f32),
            pltpu.VMEM((3, 8, rows), f32),
            pltpu.VMEM((3, bands, rows), f32),
            pltpu.VMEM((8, every), f32),
            pltpu.VMEM((slabs, 8, every), f32),
            pltpu.VMEM((8, 128), f32),
            pltpu.VMEM((slabs, 8, 128), f32),
            dma((5,)),
            dma((5,)),
            dma((3, CHUNKS)),
            dma((3, CHUNKS)),
            dma((3, CHUNKS)),
            dma((3, CHUNKS)),
            dma((3, slabs)),
            dma((3, slabs)),
            dma((3, slabs)),
            dma((3, slabs)),
            dma((slabs,)),
            dma((slabs,)),
            dma((slabs,)),
            dma((slabs,)),
            dma((2,)),
        ],
        compiler_params=pltpu.CompilerParams(
            collective_id=0, has_side_effects=True, vmem_limit_bytes=40 * 1024 * 1024
        ),
    )(
        occupied,
        start_guess[0],
        potential,
        perturbation,
        energy,
        fields,
    )


def local(
    occupied,
    start_guess,
    potential,
    perturbation,
    band_energy,
    beta_radial,
    beta_slope,
    atom_owner,
    atom_site,
    sphere_offset,
    displaced,
):
    slabs = lax.axis_size("dom")
    bands, cells = start_guess.shape[1:]
    atoms = atom_owner.shape[0]
    fields = atom_fields(
        slabs, cells, beta_radial, beta_slope, sphere_offset, atom_owner, atom_site, displaced
    )
    fits = bands == 8 * slabs and lax.axis_size("band") == 4 and atoms % 16 == 0 and atoms <= 112
    if fits and cells == HALO * PLANE:
        return fused(
            atoms,
            occupied,
            start_guess,
            potential[None, :],
            perturbation,
            band_energy[:, None],
            fields,
        )
    answer, residual = plain(
        occupied,
        start_guess[0],
        potential[None, :],
        perturbation,
        band_energy[:, None],
        fields[:atoms],
        fields[atoms : atoms + 8],
        jnp.asarray(plane_matrix()),
    )
    return answer[None], residual[None]


def solution(mesh):
    return jax.shard_map(
        local,
        mesh=mesh,
        in_specs=(
            P("band", "dom"),
            P(None, "band", "dom"),
            P("dom"),
            P(None, "dom"),
            P("band"),
            P(),
            P(),
            P(),
            P(),
            P(),
            P(),
        ),
        out_specs=(P(None, "band", "dom"), P(None, "band", "dom")),
        check_vma=False,
    )
```
